32 devices in a mesh: leaf: 2 (over x), rows: 16 (over z, y, core).
Axes of the slice: x: 2, y: 2, z: 4, core: 2. Of those that a mesh axis runs over, the one named last changes fastest.
Arguments:
- features: bfloat16 [262144, 256], P(('leaf', 'rows')), parts along dimension 0, may hold values from -80 to 80
- node_ids: int32 [262144], P(('leaf', 'rows')), parts along dimension 0, may hold values from -1 to 15, as said below
- labels: int32 [262144], P(('leaf', 'rows')), parts along dimension 0, may hold values from 0 to 15
- owners: int32 [32], P('leaf'), parts along dimension 0, may hold values from 0 to 15, each once
Outputs:
- hyperplanes: float32 [32, 16, 256], P(('leaf', 'rows')), parts along dimension 0
- scores: float32 [16, 262144], P(None, ('leaf', 'rows')), parts along dimension 1
The draws below stay inside these ranges and needn't reach their ends.
There are 2 independent parts, one for each index of `leaf`. The reference program is written for one: setup_inputs(seed, part) draws one part's arguments, and reference() takes and returns one part's arrays. A program takes and returns all parts, laid end to end along the dimension named above; each array names one. Nothing has to cross between parts.
Inputs may be any that keep to these rules, and one draw needn't show every extreme that they name: `node_ids`: on rows device d, row p of node n's segment (local row n * 512 + p) holds n or -1; the live rows of a segment come first and there is at least one; some segment of every device is full. Each node number appears once in owners; node n is owned by the device of rows with index owners[n].
All inputs are finite; a program needn't handle non-finite values.
Results may differ from the reference program's by a relative error of at most 0.0035.
Values may be sent and summed in bfloat16 or wider, within the bound.
No kernel may reach another device: no remote copies, remote signals or barrier semaphores. Data moves between devices by JAX's collectives and lax.ppermute only.
A program may use at most 128 MiB of HBM per device.

```python
import math
import jax
import jax.numpy as jnp
from jax import lax

F = 256
CLASSES = 16
ROW_DEV = 8192
NODES = 16
SEG = 512
TOTAL_ROWS = 131072
N_ROWS = 16


def label_draw(key):
    positions = jnp.arange(TOTAL_ROWS, dtype=jnp.int32)
    node_of = positions % ROW_DEV // SEG
    present = jax.random.randint(jax.random.fold_in(key, 11), (NODES, CLASSES), 0, 4) > 0
    forced = jnp.arange(CLASSES, dtype=jnp.int32)[None, :] == (jnp.arange(NODES, dtype=jnp.int32) % CLASSES)[:, None]
    present = (present | forced).astype(jnp.int32)
    noise = jax.random.randint(jax.random.fold_in(key, 12), (TOTAL_ROWS, CLASSES), 0, 1 << 20)
    ranked = noise + present[node_of] * (1 << 21)
    return jnp.argmax(ranked, axis=1).astype(jnp.int32)


def draw_labels(key, part):
    return label_draw(jax.random.fold_in(key, 5))


def draw_features(key, part):
    marks = label_draw(jax.random.fold_in(key, 5))
    base = jax.random.normal(jax.random.fold_in(key, 21), (TOTAL_ROWS, F), jnp.float32)
    mixing = jnp.eye(F, dtype=jnp.float32) + 0.5 * jax.random.normal(jax.random.fold_in(key, 22), (F, F), jnp.float32) / math.sqrt(F)
    centres = jax.random.normal(jax.random.fold_in(key, 23), (CLASSES, F), jnp.float32)
    values = jnp.dot(base, mixing, precision=lax.Precision.HIGHEST) + centres[marks]
    return jnp.clip(values, -80.0, 80.0).astype(jnp.bfloat16)


def draw_node_ids(key, part):
    device = jnp.arange(N_ROWS, dtype=jnp.int32)
    ceiling = jnp.maximum((SEG + 2 * SEG * device // max(N_ROWS - 1, 1)) // 3, 1)
    lengths = jax.random.randint(jax.random.fold_in(key, 31), (N_ROWS, NODES), 1, ceiling[:, None] + 1)
    filled = jnp.arange(NODES, dtype=jnp.int32)[None, :] == (device % NODES)[:, None]
    lengths = jnp.where(filled, SEG, lengths)
    within = jnp.arange(SEG, dtype=jnp.int32)
    node_index = jnp.broadcast_to(jnp.arange(NODES, dtype=jnp.int32)[None, :, None], (N_ROWS, NODES, SEG))
    result = jnp.where(within[None, None, :] < lengths[:, :, None], node_index, -1)
    return result.reshape(TOTAL_ROWS).astype(jnp.int32)


def setup_inputs(seed: int = 0, part: int = 0) -> dict:
    keys = jax.random.split(jax.random.key(seed), 5)
    own_keys = jax.random.split(jax.random.fold_in(keys[4], part), 5)
    return {
        "features": draw_features(jax.random.fold_in(jax.random.fold_in(keys[4], part), 71), part),
        "node_ids": draw_node_ids(jax.random.fold_in(jax.random.fold_in(keys[4], part), 71), part),
        "labels": draw_labels(jax.random.fold_in(jax.random.fold_in(keys[4], part), 71), part),
        "owners": jax.random.permutation(own_keys[3], NODES).astype(jnp.int32),
    }


ridge_term = 0.1

def solve_nodes(scatter, sums, counts):
    totals = jnp.sum(counts, axis=1)
    centers = jnp.sum(sums, axis=1) / totals[:, None]
    scaled = sums / jnp.maximum(counts, 1.0)[:, :, None]
    within = scatter - jnp.einsum('ncf,ncg->nfg', scaled, sums, precision=lax.Precision.HIGHEST)
    identity = jnp.eye(scatter.shape[-1], dtype=jnp.float32)
    system = within / totals[:, None, None] + ridge_term * identity
    shifts = (sums - counts[:, :, None] * centers[:, None, :]) / totals[:, None, None]
    factor = jnp.linalg.cholesky(system)
    planes = jax.vmap(lambda lower, right: jax.scipy.linalg.cho_solve((lower, True), right.T).T)(factor, shifts)
    offsets = -jnp.einsum('ncf,nf->nc', planes, centers, precision=lax.Precision.HIGHEST)
    return (planes, offsets)

def reference(features, node_ids, labels, owners):
    blocks = features.reshape(N_ROWS, NODES, SEG, F)
    live_rows = node_ids.reshape(N_ROWS, NODES, SEG) == jnp.arange(NODES, dtype=jnp.int32)[None, :, None]
    marks = labels.reshape(N_ROWS, NODES, SEG)
    classes = jnp.arange(CLASSES, dtype=jnp.int32)

    def one_node(index):
        chosen = lax.dynamic_index_in_dim(blocks, index, 1, keepdims=False)
        alive = lax.dynamic_index_in_dim(live_rows, index, 1, keepdims=False).reshape(-1)
        tags = lax.dynamic_index_in_dim(marks, index, 1, keepdims=False).reshape(-1)
        values = jnp.where(alive[:, None], chosen.reshape(-1, F).astype(jnp.float32), 0.0)
        onehot = ((tags[None, :] == classes[:, None]) & alive[None, :]).astype(jnp.float32)
        scatter = jnp.dot(values.T.astype(jnp.float32), values.astype(jnp.float32), preferred_element_type=jnp.float32, precision=lax.Precision.HIGHEST)
        sums = jnp.dot(onehot.astype(jnp.float32), values.astype(jnp.float32), preferred_element_type=jnp.float32, precision=lax.Precision.HIGHEST)
        counts = jnp.sum(onehot, axis=1)
        return (scatter, sums, counts)
    scatter, sums, counts = lax.map(one_node, jnp.arange(NODES, dtype=jnp.int32))
    planes, offsets = solve_nodes(scatter, sums, counts)
    inverse = jnp.zeros((NODES,), jnp.int32).at[owners].set(jnp.arange(NODES, dtype=jnp.int32))
    hyperplanes = jnp.take(planes, inverse, axis=0)
    rounded = lax.optimization_barrier(planes.astype(jnp.bfloat16)).astype(jnp.float32)

    def one_device(pair):
        chosen, alive = pair
        result = jnp.einsum('ncf,nsf->cns', rounded, chosen.astype(jnp.float32), precision=lax.Precision.HIGHEST)
        result = result + offsets.T[:, :, None]
        return jnp.where(alive[None], result, 0.0)
    scores = lax.map(one_device, (blocks, live_rows))
    scores = jnp.transpose(scores, (1, 0, 2, 3)).reshape(CLASSES, TOTAL_ROWS)
    return (hyperplanes, scores)
```

```python
import functools

import jax
import jax.numpy as jnp
from jax import lax
from jax.experimental import pallas as pl
from jax.experimental.pallas import tpu as pltpu
from jax.sharding import PartitionSpec as P

CLASSES = 16
RIDGE = 0.1
PANEL = 16
LANES = 128
HIGH = lax.Precision.HIGHEST


def split(x):
    hi = x.astype(jnp.bfloat16)
    rest = x - hi.astype(jnp.float32)
    mid = rest.astype(jnp.bfloat16)
    low = (rest - mid.astype(jnp.float32)).astype(jnp.bfloat16)
    return hi, mid, low


def over_rows(a, b):
    return lax.dot_general(a, b, (((0,), (0,)), ((), ())), preferred_element_type=jnp.float32)


def wide_over_rows(a, b):
    a1, a2, a3 = split(a)
    b1, b2, b3 = split(b)
    return over_rows(
        jnp.concatenate([a1, a1, a2, a2, a1, a3], axis=0), jnp.concatenate([b1, b2, b1, b2, b3, b1], axis=0)
    )


def reverse(number, bits):
    return sum((((number >> b) & 1) << (bits - 1 - b)) for b in range(bits))


def sums_kernel(bits, owners, features, node_ids, labels, kept, sent):
    node = pl.program_id(0)
    segment, size = features.shape
    half = size // 2
    here = pl.ds(pl.multiple_of(node * segment, segment), segment)
    alive = node_ids[here].reshape(1, segment) == node
    marks = labels[here].reshape(1, segment)
    classes = lax.broadcasted_iota(jnp.int32, (CLASSES, segment), 0)
    hot = jnp.where((marks == classes) & alive, 1.0, 0.0)
    length = jnp.sum(jnp.where(alive, 1.0, 0.0), axis=1, keepdims=True).astype(jnp.int32)
    rows = lax.broadcasted_iota(jnp.int32, (segment, size), 0)
    masked = jnp.where(rows < length, features[...], jnp.zeros((), jnp.bfloat16))
    moment = over_rows(masked, masked)
    sums = jnp.dot(hot.astype(jnp.bfloat16), masked, preferred_element_type=jnp.float32)
    counts = jnp.sum(hot, axis=1, keepdims=True)
    ci = lax.broadcasted_iota(jnp.int32, (CLASSES, half), 0)
    cj = lax.broadcasted_iota(jnp.int32, (CLASSES, half), 1)
    count_row = jnp.sum(jnp.where(ci == cj, counts, 0.0), axis=0, keepdims=True)
    i = lax.broadcasted_iota(jnp.int32, (half, half), 0)
    j = lax.broadcasted_iota(jnp.int32, (half, half), 1)
    last = moment[half:, half:]
    mixed = jnp.where(i <= j, moment[:half, :half], last)
    diagonal = jnp.sum(jnp.where(i == j, last, 0.0), axis=0, keepdims=True)
    ti = lax.broadcasted_iota(jnp.int32, (8, half), 0)
    tail = jnp.where(ti == 0, diagonal, jnp.where(ti == 1, count_row, 0.0))

    apart = owners[node] ^ lax.axis_index("rows")
    place = reverse(apart & -2, bits)

    def store(out):
        out[place, 0:half] = moment[:half, half:]
        out[place, half : 2 * half] = mixed
        out[place, 2 * half : 2 * half + CLASSES] = sums[:, :half]
        out[place, 2 * half + CLASSES : 2 * half + 2 * CLASSES] = sums[:, half:]
        out[place, 2 * half + 2 * CLASSES :] = tail

    @pl.when((apart & 1) == 0)
    def _():
        store(kept)

    @pl.when((apart & 1) == 1)
    def _():
        store(sent)


def local_sums(features, node_ids, labels, owners, bits):
    row_count, size = features.shape
    nodes = owners.shape[0]
    segment = row_count // nodes
    block = (nodes // 2, size + 2 * CLASSES + 8, size // 2)
    out = jax.ShapeDtypeStruct(block, jnp.float32)
    whole = pl.BlockSpec(block, lambda n, o: (0, 0, 0))
    return pl.pallas_call(
        functools.partial(sums_kernel, bits),
        out_shape=(out, out),
        grid_spec=pltpu.PrefetchScalarGridSpec(
            num_scalar_prefetch=1,
            grid=(nodes,),
            in_specs=[
                pl.BlockSpec((segment, size), lambda n, o: (n, 0)),
                pl.BlockSpec((row_count,), lambda n, o: (0,)),
                pl.BlockSpec((row_count,), lambda n, o: (0,)),
            ],
            out_specs=(whole, whole),
        ),
        compiler_params=pltpu.CompilerParams(vmem_limit_bytes=48 << 20),
        name="local_sums",
    )(owners, features, node_ids, labels)


def sweep(matrix, size):
    lanes=lax.broadcasted_iota(jnp.int32,(1,size),1)
    rows=lax.broadcasted_iota(jnp.int32,(PANEL,1),0)
    lane_id=lax.broadcasted_iota(jnp.int32,(PANEL,size),1)
    row_id=lax.broadcasted_iota(jnp.int32,(PANEL,size),0)
    panel=matrix[0:PANEL,:]
    for first in range(0,size,PANEL):
        last=first+PANEL
        inside=(lanes>=first)&(lanes<last)
        p1,p2,p3=split(panel)
        left=jnp.concatenate([p1,p1,p2,p2,p1,p3],axis=0)
        column=[jnp.broadcast_to(panel[:,first+c:first+c+1],(PANEL,128)) for c in range(PANEL)]
        work=jnp.where(inside,jnp.where(lane_id==row_id+first,-1.0,0.0),panel)
        scale=jnp.zeros((PANEL,128),jnp.float32)
        for k in range(PANEL):
            here=rows==k
            inverse=1.0/jnp.broadcast_to(column[k][k:k+1,:],(PANEL,128))
            factor=jnp.where(here,0.0,column[k]*inverse)
            scale=jnp.where(here,inverse,scale)
            for c in range(k+1,PANEL):
                column[c]=column[c]-factor*column[c][k:k+1,:]
            work=work-jnp.concatenate([factor]*(size//128),axis=1)*work[k:k+1,:]
        work=work*jnp.concatenate([scale]*(size//128),axis=1)
        w1,w2,w3=split(work)
        right=jnp.concatenate([w1,w2,w1,w2,w3,w1],axis=0)
        if last<size:
            base=last//128*128
            edge=over_rows(left[:,base:base+128],right)
            panel=jnp.where(inside,0.0,matrix[last:last+PANEL,:])-edge[last-base:last-base+PANEL,:]
        update=over_rows(left,right)
        matrix[...]=jnp.where(inside,0.0,matrix[...])-update
        matrix[first:last,:]=work
def solve_kernel(size, kept, came, planes, message, matrix):
    half=size//2
    total_block=kept[0]+came[0]
    cross=total_block[0:half]
    mixed=total_block[half:2*half]
    sums=jnp.concatenate([total_block[2*half:2*half+CLASSES],total_block[2*half+CLASSES:2*half+2*CLASSES]],axis=1)
    at=2*half+2*CLASSES
    diagonal=total_block[at:at+1]
    count_row=total_block[at+1:at+2]
    i=lax.broadcasted_iota(jnp.int32,(half,half),0); j=lax.broadcasted_iota(jnp.int32,(half,half),1)
    ci=lax.broadcasted_iota(jnp.int32,(CLASSES,half),0); cj=lax.broadcasted_iota(jnp.int32,(CLASSES,half),1)
    counts=jnp.sum(jnp.where(ci==cj,count_row,0.0),axis=1,keepdims=True)
    total=jnp.sum(counts,axis=0,keepdims=True)
    centers=jnp.sum(sums,axis=0,keepdims=True)/total
    scaled=sums/jnp.maximum(counts,1.0)
    shifts=(sums-counts*centers)/total
    between=wide_over_rows(sums,scaled)
    upper=jnp.where(i<j,mixed,0.0)
    lower=jnp.where(i>j,mixed,0.0)
    ridge=jnp.where(i==j,RIDGE,0.0)
    a11=upper+upper.T+jnp.where(i==j,mixed,0.0)
    a22=lower+lower.T+jnp.where(i==j,diagonal,0.0)
    matrix[0:half,0:half]=(a11-between[0:half,0:half])/total+ridge
    matrix[0:half,half:]=(cross-between[0:half,half:])/total
    matrix[half:,0:half]=(cross.T-between[half:,0:half])/total
    matrix[half:,half:]=(a22-between[half:,half:])/total+ridge
    sweep(matrix,size)
    result=-jnp.dot(shifts,matrix[...],precision=HIGH,preferred_element_type=jnp.float32)
    planes[0]=result
    offsets=-jnp.sum(result*centers,axis=1,keepdims=True)
    o1,o2,o3=split(offsets)
    message[0,:,0:size]=result.astype(jnp.bfloat16)
    lane=lax.broadcasted_iota(jnp.int32,(CLASSES,128),1)
    message[0,:,size:]=jnp.where(lane==0,o1.astype(jnp.float32),jnp.where(lane==1,o2.astype(jnp.float32),jnp.where(lane==2,o3.astype(jnp.float32),0.0))).astype(jnp.bfloat16)
def solve(kept,came,size):
    return pl.pallas_call(functools.partial(solve_kernel,size),
        out_shape=(jax.ShapeDtypeStruct((1,CLASSES,size),jnp.float32),jax.ShapeDtypeStruct((1,CLASSES,size+128),jnp.bfloat16)),
        scratch_shapes=[pltpu.VMEM((size,size),jnp.float32)],
        compiler_params=pltpu.CompilerParams(vmem_limit_bytes=32<<20),
        name="solve")(kept,came)


def scores_kernel(bits, owners, features, node_ids, messages, scores):
    node = pl.program_id(0)
    segment, size = features.shape
    here = pl.ds(pl.multiple_of(node * segment, segment), segment)
    alive = node_ids[here].reshape(1, segment) == node
    message = messages[reverse(owners[node] ^ lax.axis_index("rows"), bits)]
    offsets = jnp.sum(message[:, size:].astype(jnp.float32), axis=1, keepdims=True)
    result = lax.dot_general(
        message[:, :size], features[...], (((1,), (1,)), ((), ())), preferred_element_type=jnp.float32
    )
    scores[...] = jnp.where(alive, result + offsets, 0.0)


def all_scores(features, node_ids, owners, messages, bits):
    row_count, size = features.shape
    nodes = owners.shape[0]
    segment = row_count // nodes
    return pl.pallas_call(
        functools.partial(scores_kernel, bits),
        out_shape=jax.ShapeDtypeStruct((CLASSES, row_count), jnp.float32),
        grid_spec=pltpu.PrefetchScalarGridSpec(
            num_scalar_prefetch=1,
            grid=(nodes,),
            in_specs=[
                pl.BlockSpec((segment, size), lambda n, o: (n, 0)),
                pl.BlockSpec((row_count,), lambda n, o: (0,)),
                pl.BlockSpec(messages.shape, lambda n, o: (0, 0, 0)),
            ],
            out_specs=pl.BlockSpec((CLASSES, segment), lambda n, o: (0, n)),
        ),
        compiler_params=pltpu.CompilerParams(vmem_limit_bytes=32 << 20),
        name="all_scores",
    )(owners, features, node_ids, messages)


def on_device(ranks, features, node_ids, labels, owners):
    size = features.shape[1]
    bits = ranks.bit_length() - 1

    def swap(x, distance):
        return lax.ppermute(x, "rows", [(r, r ^ distance) for r in range(ranks)])

    kept, sent = local_sums(features, node_ids, labels, owners, bits)
    came = swap(sent, 1)
    for b in range(1, bits):
        middle = kept.shape[0] // 2
        sent = kept[middle:] + came[middle:]
        next_came = swap(sent, 1 << b)
        kept = kept[:middle] + came[:middle]
        came = next_came
    planes, held = solve(kept, came, size)
    for b in reversed(range(bits)):
        held = jnp.concatenate([held, swap(held, 1 << b)], axis=0)
    return planes, all_scores(features, node_ids, owners, held, bits)


def solution(mesh):
    ranks = mesh.shape["rows"]
    in_specs = (P(("leaf", "rows"), None), P(("leaf", "rows")), P(("leaf", "rows")), P("leaf"))
    out_specs = (P(("leaf", "rows"), None, None), P(None, ("leaf", "rows")))
    return jax.shard_map(
        functools.partial(on_device, ranks), mesh=mesh, in_specs=in_specs, out_specs=out_specs, check_vma=False
    )
```

```python
import functools

import jax
import jax.numpy as jnp
from jax import lax
from jax.experimental import pallas as pl
from jax.experimental.pallas import tpu as pltpu
from jax.sharding import PartitionSpec as P

CLASSES = 16
RIDGE = 0.1
PANEL = 16
LANES = 128
HIGH = lax.Precision.HIGHEST


def split(x):
    hi = x.astype(jnp.bfloat16)
    rest = x - hi.astype(jnp.float32)
    mid = rest.astype(jnp.bfloat16)
    low = (rest - mid.astype(jnp.float32)).astype(jnp.bfloat16)
    return hi, mid, low


def over_rows(a, b):
    return lax.dot_general(a, b, (((0,), (0,)), ((), ())), preferred_element_type=jnp.float32)


def wide_over_rows(a, b):
    a1, a2, a3 = split(a)
    b1, b2, b3 = split(b)
    return over_rows(
        jnp.concatenate([a1, a1, a2, a2, a1, a3], axis=0), jnp.concatenate([b1, b2, b1, b2, b3, b1], axis=0)
    )


def reverse(number, bits):
    return sum((((number >> b) & 1) << (bits - 1 - b)) for b in range(bits))


def exchange_orders(bits):
    plain = list(range(1, bits))
    return plain, plain if bits < 3 else [2, 1] + plain[2:]


def packed_sums(x, alive, marks):
    segment, size = x.shape
    half = size // 2
    classes = lax.broadcasted_iota(jnp.int32, (CLASSES, segment), 0)
    hot = jnp.where((marks == classes) & alive, 1.0, 0.0)
    counts = jnp.sum(hot, axis=1, keepdims=True)
    live = jnp.where(alive, 1.0, 0.0).astype(jnp.bfloat16)
    left = jnp.concatenate([x.T * live, hot.astype(jnp.bfloat16)], axis=0)
    both = jnp.dot(left, x, preferred_element_type=jnp.float32)
    moment, sums = both[:size], both[size:]
    ci = lax.broadcasted_iota(jnp.int32, (CLASSES, half), 0)
    cj = lax.broadcasted_iota(jnp.int32, (CLASSES, half), 1)
    count_row = jnp.sum(jnp.where(ci == cj, counts, 0.0), axis=0, keepdims=True)
    i = lax.broadcasted_iota(jnp.int32, (half, half), 0)
    j = lax.broadcasted_iota(jnp.int32, (half, half), 1)
    last = moment[half:, half:]
    mixed = jnp.where(i <= j, moment[:half, :half], last)
    diagonal = jnp.sum(jnp.where(i == j, last, 0.0), axis=0, keepdims=True)
    ti = lax.broadcasted_iota(jnp.int32, (8, half), 0)
    tail = jnp.where(ti == 0, diagonal, jnp.where(ti == 1, count_row, 0.0))
    return moment[:half, half:], mixed, sums, tail


def sums_kernel(
    bits, group, owners, features, node_ids, labels, kept, sent, listed, rows, ids, marks, row_sems, id_sem, mark_sem
):
    me = lax.axis_index("rows")
    nodes = owners.shape[0]
    count, segment, size = rows.shape
    half = size // 2
    copy_ids = pltpu.make_async_copy(node_ids, ids, id_sem)
    copy_marks = pltpu.make_async_copy(labels, marks, mark_sem)
    copy_ids.start()
    copy_marks.start()

    def segment_of(node):
        return pl.ds(pl.multiple_of(node * segment, segment), segment)

    def fetch(q, node):
        return pltpu.make_async_copy(features.at[segment_of(node)], rows.at[q], row_sems.at[q])

    even_order, odd_order = exchange_orders(bits)
    for node in range(nodes):
        owner = owners[node]
        apart = owner ^ me

        def position(order, apart=apart):
            return sum(((apart >> b) & 1) << (bits - 2 - t) for t, b in enumerate(order))

        place = jnp.where((owner & 1) == 1, position(odd_order), position(even_order))
        slot = (place & (count // 2 - 1)) + (apart & 1) * (count // 2)

        @pl.when((place >> (bits - 2)) == group)
        def _(slot=slot, node=node):
            listed[slot] = node
            fetch(slot, node).start()

    copy_ids.wait()
    copy_marks.wait()

    def fill(out, base):
        def step(q, carry):
            node = listed[base + q]
            fetch(base + q, node).wait()
            here = segment_of(node)
            alive = ids[here].reshape(1, segment) == node
            cross, mixed, sums, tail = packed_sums(rows[base + q], alive, marks[here].reshape(1, segment))
            out[q, 0:half] = cross
            out[q, half : 2 * half] = mixed
            out[q, 2 * half : 2 * half + CLASSES] = sums[:, :half]
            out[q, 2 * half + CLASSES : 2 * half + 2 * CLASSES] = sums[:, half:]
            out[q, 2 * half + 2 * CLASSES :] = tail
            return carry

        lax.fori_loop(0, count // 2, step, 0)

    fill(sent, count // 2)
    fill(kept, 0)


def local_sums(features, node_ids, labels, owners, bits, group):
    row_count, size = features.shape
    nodes = owners.shape[0]
    segment = row_count // nodes
    count = nodes // 2
    out = jax.ShapeDtypeStruct((count // 2, size + 2 * CLASSES + 8, size // 2), jnp.float32)
    far = pl.BlockSpec(memory_space=pltpu.HBM)
    near = pl.BlockSpec(memory_space=pltpu.VMEM)
    return pl.pallas_call(
        functools.partial(sums_kernel, bits, group),
        out_shape=(out, out),
        in_specs=[pl.BlockSpec(memory_space=pltpu.SMEM), far, far, far],
        out_specs=(near, near),
        scratch_shapes=[
            pltpu.SMEM((count,), jnp.int32),
            pltpu.VMEM((count, segment, size), jnp.bfloat16),
            pltpu.VMEM((row_count,), jnp.int32),
            pltpu.VMEM((row_count,), jnp.int32),
            pltpu.SemaphoreType.DMA((count,)),
            pltpu.SemaphoreType.DMA,
            pltpu.SemaphoreType.DMA,
        ],
        compiler_params=pltpu.CompilerParams(vmem_limit_bytes=58 << 20),
        cost_estimate=pl.CostEstimate(
            flops=row_count * size * size, bytes_accessed=row_count * size, transcendentals=0
        ),
        name="local_sums",
    )(owners, features, node_ids, labels)


def sweep(matrix, size):
    lanes=lax.broadcasted_iota(jnp.int32,(1,size),1)
    rows=lax.broadcasted_iota(jnp.int32,(PANEL,1),0)
    lane_id=lax.broadcasted_iota(jnp.int32,(PANEL,size),1)
    row_id=lax.broadcasted_iota(jnp.int32,(PANEL,size),0)
    panel=matrix[0:PANEL,:]
    for first in range(0,size,PANEL):
        last=first+PANEL
        inside=(lanes>=first)&(lanes<last)
        p1,p2,p3=split(panel)
        left=jnp.concatenate([p1,p1,p2,p2,p1,p3],axis=0)
        column=[jnp.broadcast_to(panel[:,first+c:first+c+1],(PANEL,128)) for c in range(PANEL)]
        work=jnp.where(inside,jnp.where(lane_id==row_id+first,-1.0,0.0),panel)
        scale=jnp.zeros((PANEL,128),jnp.float32)
        for k in range(PANEL):
            here=rows==k
            inverse=1.0/jnp.broadcast_to(column[k][k:k+1,:],(PANEL,128))
            factor=jnp.where(here,0.0,column[k]*inverse)
            scale=jnp.where(here,inverse,scale)
            for c in range(k+1,PANEL):
                column[c]=column[c]-factor*column[c][k:k+1,:]
            work=work-jnp.concatenate([factor]*(size//128),axis=1)*work[k:k+1,:]
        work=work*jnp.concatenate([scale]*(size//128),axis=1)
        w1,w2,w3=split(work)
        right=jnp.concatenate([w1,w2,w1,w2,w3,w1],axis=0)
        if last<size:
            base=last//128*128
            edge=over_rows(left[:,base:base+128],right)
            panel=jnp.where(inside,0.0,matrix[last:last+PANEL,:])-edge[last-base:last-base+PANEL,:]
        update=over_rows(left,right)
        matrix[...]=jnp.where(inside,0.0,matrix[...])-update
        matrix[first:last,:]=work
def solve_kernel(size, kept, came, planes, message, matrix):
    half=size//2
    total_block=kept[0]+came[0]
    cross=total_block[0:half]
    mixed=total_block[half:2*half]
    sums=jnp.concatenate([total_block[2*half:2*half+CLASSES],total_block[2*half+CLASSES:2*half+2*CLASSES]],axis=1)
    at=2*half+2*CLASSES
    diagonal=total_block[at:at+1]
    count_row=total_block[at+1:at+2]
    i=lax.broadcasted_iota(jnp.int32,(half,half),0); j=lax.broadcasted_iota(jnp.int32,(half,half),1)
    ci=lax.broadcasted_iota(jnp.int32,(CLASSES,half),0); cj=lax.broadcasted_iota(jnp.int32,(CLASSES,half),1)
    counts=jnp.sum(jnp.where(ci==cj,count_row,0.0),axis=1,keepdims=True)
    total=jnp.sum(counts,axis=0,keepdims=True)
    centers=jnp.sum(sums,axis=0,keepdims=True)/total
    scaled=sums/jnp.maximum(counts,1.0)
    shifts=(sums-counts*centers)/total
    between=wide_over_rows(sums,scaled)
    upper=jnp.where(i<j,mixed,0.0)
    lower=jnp.where(i>j,mixed,0.0)
    ridge=jnp.where(i==j,RIDGE,0.0)
    a11=upper+upper.T+jnp.where(i==j,mixed,0.0)
    a22=lower+lower.T+jnp.where(i==j,diagonal,0.0)
    matrix[0:half,0:half]=(a11-between[0:half,0:half])/total+ridge
    matrix[0:half,half:]=(cross-between[0:half,half:])/total
    matrix[half:,0:half]=(cross.T-between[half:,0:half])/total
    matrix[half:,half:]=(a22-between[half:,half:])/total+ridge
    sweep(matrix,size)
    result=-jnp.dot(shifts,matrix[...],precision=HIGH,preferred_element_type=jnp.float32)
    planes[0]=result
    offsets=-jnp.sum(result*centers,axis=1,keepdims=True)
    o1,o2,o3=split(offsets)
    message[0,:,0:size]=result.astype(jnp.bfloat16)
    lane=lax.broadcasted_iota(jnp.int32,(CLASSES,128),1)
    message[0,:,size:]=jnp.where(lane==0,o1.astype(jnp.float32),jnp.where(lane==1,o2.astype(jnp.float32),jnp.where(lane==2,o3.astype(jnp.float32),0.0))).astype(jnp.bfloat16)
def solve(kept,came,size):
    return pl.pallas_call(functools.partial(solve_kernel,size),
        out_shape=(jax.ShapeDtypeStruct((1,CLASSES,size),jnp.float32),jax.ShapeDtypeStruct((1,CLASSES,size+128),jnp.bfloat16)),
        scratch_shapes=[pltpu.VMEM((size,size),jnp.float32)],
        compiler_params=pltpu.CompilerParams(vmem_limit_bytes=32<<20),
        name="solve")(kept,came)


def scores_kernel(bits, group, owners, features, node_ids, messages, scores):
    size = features.shape[1]
    segment = scores.shape[1] // group
    for g in range(group):
        node = pl.program_id(0) * group + g
        here = pl.ds(pl.multiple_of(node * segment, segment), segment)
        alive = node_ids[here].reshape(1, segment) == node
        message = messages[reverse(owners[node] ^ lax.axis_index("rows"), bits)]
        offsets = jnp.sum(message[:, size:].astype(jnp.float32), axis=1, keepdims=True)
        result = lax.dot_general(
            message[:, :size], features[here, :], (((1,), (1,)), ((), ())), preferred_element_type=jnp.float32
        )
        scores[:, g * segment : (g + 1) * segment] = jnp.where(alive, result + offsets, 0.0)


def all_scores(features, node_ids, owners, messages, bits):
    row_count, size = features.shape
    nodes = owners.shape[0]
    segment = row_count // nodes
    group = nodes // 2
    near = pl.BlockSpec(memory_space=pltpu.VMEM)
    return pl.pallas_call(
        functools.partial(scores_kernel, bits, group),
        out_shape=jax.ShapeDtypeStruct((CLASSES, row_count), jnp.float32),
        grid=(nodes // group,),
        in_specs=[pl.BlockSpec(memory_space=pltpu.SMEM), near, near, near],
        out_specs=pl.BlockSpec((CLASSES, segment * group), lambda n: (0, n)),
        compiler_params=pltpu.CompilerParams(vmem_limit_bytes=32 << 20),
        name="all_scores",
    )(owners, features, node_ids, messages)


def on_device(ranks, features, node_ids, labels, owners):
    size = features.shape[1]
    bits = ranks.bit_length() - 1
    orders = exchange_orders(bits)

    def swap(x, distances):
        return lax.ppermute(x, "rows", [(r, r ^ distances[r & 1]) for r in range(ranks)])

    def halving(x, step):
        return swap(x, [1 << order[step] for order in orders])

    kept, sent = local_sums(features, node_ids, labels, owners, bits, 1)
    sent = kept + swap(sent, (1, 1))
    sent, later_owners = lax.optimization_barrier((sent, owners))
    came = halving(sent, 0)
    kept, sent = local_sums(features, node_ids, labels, later_owners, bits, 0)
    kept = (kept, swap(sent, (1, 1)))
    for step in range(1, bits - 1):
        middle = came.shape[0] // 2
        sent = sum(k[middle:] for k in kept) + came[middle:]
        next_came = halving(sent, step)
        kept = (sum(k[:middle] for k in kept) + came[:middle],)
        came = next_came
    planes, held = solve(kept[0], came, size)
    for b in reversed(range(bits)):
        held = jnp.concatenate([held, swap(held, (1 << b, 1 << b))], axis=0)
    return planes, all_scores(features, node_ids, owners, held, bits)


def solution(mesh):
    ranks = mesh.shape["rows"]
    in_specs = (P(("leaf", "rows"), None), P(("leaf", "rows")), P(("leaf", "rows")), P("leaf"))
    out_specs = (P(("leaf", "rows"), None, None), P(None, ("leaf", "rows")))
    return jax.shard_map(
        functools.partial(on_device, ranks), mesh=mesh, in_specs=in_specs, out_specs=out_specs, check_vma=False
    )
```

```python
import functools

import jax
import jax.numpy as jnp
from jax import lax
from jax.experimental import pallas as pl
from jax.experimental.pallas import tpu as pltpu
from jax.sharding import PartitionSpec as P

CLASSES = 16
RIDGE = 0.1
PANEL = 16
LANES = 128
HIGH = lax.Precision.HIGHEST


def split(x):
    hi = x.astype(jnp.bfloat16)
    rest = x - hi.astype(jnp.float32)
    mid = rest.astype(jnp.bfloat16)
    low = (rest - mid.astype(jnp.float32)).astype(jnp.bfloat16)
    return hi, mid, low


def over_rows(a, b):
    return lax.dot_general(a, b, (((0,), (0,)), ((), ())), preferred_element_type=jnp.float32)


def wide_over_rows(a, b):
    a1, a2, a3 = split(a)
    b1, b2, b3 = split(b)
    return over_rows(
        jnp.concatenate([a1, a1, a2, a2, a1, a3], axis=0), jnp.concatenate([b1, b2, b1, b2, b3, b1], axis=0)
    )


def exchange_orders(bits):
    plain = list(range(1, bits))
    return plain, plain if bits < 3 else [2, 1] + plain[2:]


def place_of(apart, owner, bits):
    even, odd = (
        sum(((apart >> b) & 1) << (bits - 2 - t) for t, b in enumerate(order)) for order in exchange_orders(bits)
    )
    return jnp.where((owner & 1) == 1, odd, even)


def packed_sums(x, alive, marks):
    segment, size = x.shape
    half = size // 2
    classes = lax.broadcasted_iota(jnp.int32, (CLASSES, segment), 0)
    hot = jnp.where((marks == classes) & alive, 1.0, 0.0)
    counts = jnp.sum(hot, axis=1, keepdims=True)
    live = jnp.where(alive, 1.0, 0.0).astype(jnp.bfloat16)
    left = jnp.concatenate([x.T * live, hot.astype(jnp.bfloat16)], axis=0)
    both = jnp.dot(left, x, preferred_element_type=jnp.float32)
    moment, sums = both[:size], both[size:]
    ci = lax.broadcasted_iota(jnp.int32, (CLASSES, half), 0)
    cj = lax.broadcasted_iota(jnp.int32, (CLASSES, half), 1)
    count_row = jnp.sum(jnp.where(ci == cj, counts, 0.0), axis=0, keepdims=True)
    i = lax.broadcasted_iota(jnp.int32, (half, half), 0)
    j = lax.broadcasted_iota(jnp.int32, (half, half), 1)
    last = moment[half:, half:]
    mixed = jnp.where(i <= j, moment[:half, :half], last)
    diagonal = jnp.sum(jnp.where(i == j, last, 0.0), axis=0, keepdims=True)
    ti = lax.broadcasted_iota(jnp.int32, (8, half), 0)
    tail = jnp.where(ti == 0, diagonal, jnp.where(ti == 1, count_row, 0.0))
    return moment[:half, half:], mixed, sums, tail


def sums_kernel(
    bits, group, owners, features, node_ids, labels, kept, sent, listed, rows, ids, marks, row_sems, id_sem, mark_sem
):
    me = lax.axis_index("rows")
    nodes = owners.shape[0]
    count, segment, size = rows.shape
    half = size // 2
    copy_ids = pltpu.make_async_copy(node_ids, ids, id_sem)
    copy_marks = pltpu.make_async_copy(labels, marks, mark_sem)
    copy_ids.start()
    copy_marks.start()

    def segment_of(node):
        return pl.ds(pl.multiple_of(node * segment, segment), segment)

    def fetch(q, node):
        return pltpu.make_async_copy(features.at[segment_of(node)], rows.at[q], row_sems.at[q])

    for node in range(nodes):
        apart = owners[node] ^ me
        place = place_of(apart, owners[node], bits)
        slot = (place & (count // 2 - 1)) + (apart & 1) * (count // 2)

        @pl.when((place >> (bits - 2)) == group)
        def _(slot=slot, node=node):
            listed[slot] = node
            fetch(slot, node).start()

    copy_ids.wait()
    copy_marks.wait()

    def fill(out, base):
        def step(q, carry):
            node = listed[base + q]
            fetch(base + q, node).wait()
            here = segment_of(node)
            alive = ids[here].reshape(1, segment) == node
            cross, mixed, sums, tail = packed_sums(rows[base + q], alive, marks[here].reshape(1, segment))
            out[q, 0:half] = cross
            out[q, half : 2 * half] = mixed
            out[q, 2 * half : 2 * half + CLASSES] = sums[:, :half]
            out[q, 2 * half + CLASSES : 2 * half + 2 * CLASSES] = sums[:, half:]
            out[q, 2 * half + 2 * CLASSES :] = tail
            return carry

        lax.fori_loop(0, count // 2, step, 0)

    fill(sent, count // 2)
    fill(kept, 0)


def local_sums(features, node_ids, labels, owners, bits, group):
    row_count, size = features.shape
    nodes = owners.shape[0]
    segment = row_count // nodes
    count = nodes // 2
    out = pltpu.VMEM((count // 2, size + 2 * CLASSES + 8, size // 2), jnp.float32)
    far = pl.BlockSpec(memory_space=pltpu.HBM)
    near = pl.BlockSpec(memory_space=pltpu.VMEM)
    return pl.pallas_call(
        functools.partial(sums_kernel, bits, group),
        out_shape=(out, out),
        in_specs=[pl.BlockSpec(memory_space=pltpu.SMEM), far, far, far],
        out_specs=(near, near),
        scratch_shapes=[
            pltpu.SMEM((count,), jnp.int32),
            pltpu.VMEM((count, segment, size), jnp.bfloat16),
            pltpu.VMEM((row_count,), jnp.int32),
            pltpu.VMEM((row_count,), jnp.int32),
            pltpu.SemaphoreType.DMA((count,)),
            pltpu.SemaphoreType.DMA,
            pltpu.SemaphoreType.DMA,
        ],
        compiler_params=pltpu.CompilerParams(vmem_limit_bytes=32 << 20),
        cost_estimate=pl.CostEstimate(
            flops=row_count * size * size, bytes_accessed=row_count * size, transcendentals=0
        ),
        name="local_sums",
    )(*(pltpu.with_memory_space_constraint(a, pltpu.HBM) for a in (owners, features, node_ids, labels)))


def sweep(matrix, size):
    across = size // LANES
    lanes = lax.broadcasted_iota(jnp.int32, (1, size), 1)
    rows = lax.broadcasted_iota(jnp.int32, (PANEL, 1), 0)
    lane_id = lax.broadcasted_iota(jnp.int32, (PANEL, size), 1)
    row_id = lax.broadcasted_iota(jnp.int32, (PANEL, size), 0)
    odd = (lax.broadcasted_iota(jnp.int32, (PANEL, size), 0) & 1) == 1

    def spread(x, at):
        return jnp.broadcast_to(x[:, at : at + 1], (PANEL, LANES))

    def wide(x):
        return jnp.concatenate([x] * across, axis=1)

    panel = matrix[0:PANEL, :]
    for first in range(0, size, PANEL):
        last = first + PANEL
        inside = (lanes >= first) & (lanes < last)
        p1, p2, p3 = split(panel)
        left = jnp.concatenate([p1, p1, p2, p2, p1, p3], axis=0)
        column = [spread(panel, first + c) for c in range(PANEL)]
        if last < size:
            following = matrix[last : last + PANEL, :]
            ahead = [spread(following, first + c) for c in range(PANEL)]
        work = jnp.where(inside, jnp.where(lane_id == row_id + first, -1.0, 0.0), panel)
        own = jnp.zeros((PANEL, LANES), jnp.float32)
        cross = own
        for k in range(0, PANEL, 2):
            c0, c1 = column[k], column[k + 1]
            b00 = jnp.broadcast_to(c0[k : k + 1, :], (PANEL, LANES))
            b10 = jnp.broadcast_to(c0[k + 1 : k + 2, :], (PANEL, LANES))
            b11 = jnp.broadcast_to(c1[k + 1 : k + 2, :], (PANEL, LANES))
            inverse = 1.0 / (b00 * b11 - b10 * b10)
            n00, n10, n11 = b11 * inverse, -b10 * inverse, b00 * inverse
            pair = (rows == k) | (rows == k + 1)
            c0, c1 = jnp.where(pair, 0.0, c0), jnp.where(pair, 0.0, c1)
            f0, f1 = c0 * n00 + c1 * n10, c0 * n10 + c1 * n11
            own = jnp.where(rows == k, n00, jnp.where(rows == k + 1, n11, own))
            cross = jnp.where(pair, n10, cross)
            for c in range(k + 2, PANEL):
                column[c] = column[c] - f0 * column[c][k : k + 1, :] - f1 * column[c][k + 1 : k + 2, :]
            work = work - wide(f0) * work[k : k + 1, :] - wide(f1) * work[k + 1 : k + 2, :]
        other = jnp.where(odd, pltpu.roll(work, 1, 0), pltpu.roll(work, PANEL - 1, 0))
        work = work * wide(own) + other * wide(cross)
        if last < size:
            terms = [wide(ahead[c]) * work[c : c + 1, :] for c in range(PANEL)]
            while len(terms) > 1:
                terms = [terms[t] + terms[t + 1] for t in range(0, len(terms), 2)]
            panel = jnp.where(inside, 0.0, following) - terms[0]
        w1, w2, w3 = split(work)
        right = jnp.concatenate([w1, w2, w1, w2, w3, w1], axis=0)
        starts = list(range(0, size, LANES))
        needed = last + PANEL if last + PANEL < size else 0
        for base in sorted(starts, key=lambda t: not t <= needed < t + LANES):
            part = over_rows(left[:, base : base + LANES], right)
            matrix[base : base + LANES, :] = jnp.where(inside, 0.0, matrix[base : base + LANES, :]) - part
        matrix[first:last, :] = work


def solve_kernel(kept, came, planes, message, matrix):
    size = matrix.shape[0]
    half = size // 2
    packed = kept[0] + came[0]
    cross, mixed = packed[:half], packed[half:size]
    sums = jnp.concatenate([packed[size : size + CLASSES], packed[size + CLASSES : size + 2 * CLASSES]], axis=1)
    at = size + 2 * CLASSES
    diagonal, count_row = packed[at : at + 1], packed[at + 1 : at + 2]
    i = lax.broadcasted_iota(jnp.int32, (half, half), 0)
    j = lax.broadcasted_iota(jnp.int32, (half, half), 1)
    ci = lax.broadcasted_iota(jnp.int32, (CLASSES, half), 0)
    cj = lax.broadcasted_iota(jnp.int32, (CLASSES, half), 1)
    counts = jnp.sum(jnp.where(ci == cj, count_row, 0.0), axis=1, keepdims=True)
    total = jnp.sum(counts, axis=0, keepdims=True)
    centers = jnp.sum(sums, axis=0, keepdims=True) / total
    scaled = sums / jnp.maximum(counts, 1.0)
    shifts = (sums - counts * centers) / total
    between = wide_over_rows(sums, scaled)
    upper = jnp.where(i < j, mixed, 0.0)
    lower = jnp.where(i > j, mixed, 0.0)
    ridge = jnp.where(i == j, RIDGE, 0.0)
    start = upper + upper.T + jnp.where(i == j, mixed, 0.0)
    end = lower + lower.T + jnp.where(i == j, diagonal, 0.0)
    matrix[:half, :half] = (start - between[:half, :half]) / total + ridge
    matrix[:half, half:] = (cross - between[:half, half:]) / total
    matrix[half:, :half] = (cross.T - between[half:, :half]) / total
    matrix[half:, half:] = (end - between[half:, half:]) / total + ridge
    sweep(matrix, size)
    result = -jnp.dot(shifts, matrix[...], precision=HIGH, preferred_element_type=jnp.float32)
    planes[0] = result
    offsets = -jnp.sum(result * centers, axis=1, keepdims=True)
    lane = lax.broadcasted_iota(jnp.int32, (CLASSES, LANES), 1)
    parts = jnp.zeros((CLASSES, LANES), jnp.float32)
    for t, term in enumerate(split(offsets)):
        parts = jnp.where(lane == t, term.astype(jnp.float32), parts)
    message[0, :, :size] = result.astype(jnp.bfloat16)
    message[0, :, size:] = parts.astype(jnp.bfloat16)


def solve(kept, came, size):
    return pl.pallas_call(
        solve_kernel,
        out_shape=(
            jax.ShapeDtypeStruct((1, CLASSES, size), jnp.float32),
            jax.ShapeDtypeStruct((1, CLASSES, size + LANES), jnp.bfloat16),
        ),
        scratch_shapes=[pltpu.VMEM((size, size), jnp.float32)],
        compiler_params=pltpu.CompilerParams(vmem_limit_bytes=32 << 20),
        name="solve",
    )(kept, came)


def scores_kernel(bits, group, owners, features, node_ids, messages, scores):
    size = features.shape[1]
    segment = scores.shape[1] // group
    for g in range(group):
        node = pl.program_id(0) * group + g
        here = pl.ds(pl.multiple_of(node * segment, segment), segment)
        alive = node_ids[here].reshape(1, segment) == node
        owner = owners[node]
        apart = owner ^ lax.axis_index("rows")
        message = messages[place_of(apart, owner, bits) + ((apart & 1) << (bits - 1))]
        offsets = jnp.sum(message[:, size:].astype(jnp.float32), axis=1, keepdims=True)
        result = lax.dot_general(
            message[:, :size], features[here, :], (((1,), (1,)), ((), ())), preferred_element_type=jnp.float32
        )
        scores[:, g * segment : (g + 1) * segment] = jnp.where(alive, result + offsets, 0.0)


def all_scores(features, node_ids, owners, messages, bits):
    row_count, size = features.shape
    nodes = owners.shape[0]
    segment = row_count // nodes
    group = nodes // 2
    near = pl.BlockSpec(memory_space=pltpu.VMEM)
    return pl.pallas_call(
        functools.partial(scores_kernel, bits, group),
        out_shape=jax.ShapeDtypeStruct((CLASSES, row_count), jnp.float32),
        grid=(nodes // group,),
        in_specs=[pl.BlockSpec(memory_space=pltpu.SMEM), near, near, near],
        out_specs=pl.BlockSpec((CLASSES, segment * group), lambda n: (0, n)),
        compiler_params=pltpu.CompilerParams(vmem_limit_bytes=32 << 20),
        name="all_scores",
    )(owners, features, node_ids, messages)


def on_device(ranks, features, node_ids, labels, owners):
    size = features.shape[1]
    bits = ranks.bit_length() - 1
    orders = exchange_orders(bits)

    def swap(x, distances):
        return lax.ppermute(x, "rows", [(r, r ^ distances[r & 1]) for r in range(ranks)])

    def halving(x, step):
        return swap(x, [1 << order[step] for order in orders])

    kept, sent = local_sums(features, node_ids, labels, owners, bits, 1)
    sent = kept + swap(sent, (1, 1))
    sent, later_owners = lax.optimization_barrier((sent, owners))
    came = halving(sent, 0)
    kept, sent = local_sums(features, node_ids, labels, later_owners, bits, 0)
    kept = (kept, swap(sent, (1, 1)))
    for step in range(1, bits - 1):
        middle = came.shape[0] // 2
        sent = sum(k[middle:] for k in kept) + came[middle:]
        next_came = halving(sent, step)
        kept = (sum(k[:middle] for k in kept) + came[:middle],)
        came = next_came
    planes, held = solve(kept[0], came, size)
    for step in reversed(range(bits - 1)):
        held = jnp.concatenate([held, halving(held, step)], axis=0)
    held = jnp.concatenate([held, swap(held, (1, 1))], axis=0)
    return planes, all_scores(features, node_ids, owners, held, bits)


def solution(mesh):
    ranks = mesh.shape["rows"]
    in_specs = (P(("leaf", "rows"), None), P(("leaf", "rows")), P(("leaf", "rows")), P("leaf"))
    out_specs = (P(("leaf", "rows"), None, None), P(None, ("leaf", "rows")))
    return jax.shard_map(
        functools.partial(on_device, ranks), mesh=mesh, in_specs=in_specs, out_specs=out_specs, check_vma=False
    )
```

```python
import functools

import jax
import jax.numpy as jnp
from jax import lax
from jax.experimental import pallas as pl
from jax.experimental.pallas import tpu as pltpu
from jax.sharding import PartitionSpec as P

CLASSES = 16
RIDGE = 0.1
PANEL = 16
LANES = 128
HIGH = lax.Precision.HIGHEST


def split(x):
    hi = x.astype(jnp.bfloat16)
    rest = x - hi.astype(jnp.float32)
    mid = rest.astype(jnp.bfloat16)
    low = (rest - mid.astype(jnp.float32)).astype(jnp.bfloat16)
    return hi, mid, low


def over_rows(a, b):
    return lax.dot_general(a, b, (((0,), (0,)), ((), ())), preferred_element_type=jnp.float32)


def wide_over_rows(a, b):
    a1, a2, a3 = split(a)
    b1, b2, b3 = split(b)
    return over_rows(
        jnp.concatenate([a1, a1, a2, a2, a1, a3], axis=0), jnp.concatenate([b1, b2, b1, b2, b3, b1], axis=0)
    )


def exchange_orders(bits):
    plain = list(range(1, bits))
    return plain, plain if bits < 3 else [2, 1] + plain[2:]


def place_of(apart, owner, bits):
    even, odd = (
        sum(((apart >> b) & 1) << (bits - 2 - t) for t, b in enumerate(order)) for order in exchange_orders(bits)
    )
    return jnp.where((owner & 1) == 1, odd, even)


def packed_sums(x, alive, marks):
    segment, size = x.shape
    half = size // 2
    classes = lax.broadcasted_iota(jnp.int32, (CLASSES, segment), 0)
    hot = jnp.where((marks == classes) & alive, 1.0, 0.0)
    counts = jnp.sum(hot, axis=1, keepdims=True)
    live = jnp.where(alive, 1.0, 0.0).astype(jnp.bfloat16)
    left = jnp.concatenate([x.T * live, hot.astype(jnp.bfloat16)], axis=0)
    both = jnp.dot(left, x, preferred_element_type=jnp.float32)
    moment, sums = both[:size], both[size:]
    ci = lax.broadcasted_iota(jnp.int32, (CLASSES, half), 0)
    cj = lax.broadcasted_iota(jnp.int32, (CLASSES, half), 1)
    count_row = jnp.sum(jnp.where(ci == cj, counts, 0.0), axis=0, keepdims=True)
    i = lax.broadcasted_iota(jnp.int32, (half, half), 0)
    j = lax.broadcasted_iota(jnp.int32, (half, half), 1)
    last = moment[half:, half:]
    mixed = jnp.where(i <= j, moment[:half, :half], last)
    diagonal = jnp.sum(jnp.where(i == j, last, 0.0), axis=0, keepdims=True)
    ti = lax.broadcasted_iota(jnp.int32, (8, half), 0)
    tail = jnp.where(ti == 0, diagonal, jnp.where(ti == 1, count_row, 0.0))
    return moment[:half, half:], mixed, sums, tail


def packed_shape(size, blocks):
    return pltpu.VMEM((blocks, size + 2 * CLASSES + 8, size // 2), jnp.float32)


def fill(out, section, listed, rows, ids, marks, segment):
    blocks = out.shape[0]
    size = rows.shape[1]
    half = size // 2

    def step(q, carry):
        node = listed[section * blocks + q]
        here = pl.ds(pl.multiple_of(node * segment, segment), segment)
        alive = ids[here].reshape(1, segment) == node
        cross, mixed, sums, tail = packed_sums(rows[here, :], alive, marks[here].reshape(1, segment))
        out[q, 0:half] = cross
        out[q, half:size] = mixed
        out[q, size : size + CLASSES] = sums[:, :half]
        out[q, size + CLASSES : size + 2 * CLASSES] = sums[:, half:]
        out[q, size + 2 * CLASSES :] = tail
        return carry

    lax.fori_loop(0, blocks, step, 0)


def first_sums_kernel(
    bits, owners, features, node_ids, labels, sent, listed, rows, ids, marks, owner_list, row_sems, list_sem, id_sem, mark_sem
):
    nodes = owners.shape[0]
    segment = rows.shape[0] // nodes
    quarter = nodes // 4
    copies = [
        pltpu.make_async_copy(owners, owner_list, list_sem),
        pltpu.make_async_copy(node_ids, ids, id_sem),
        pltpu.make_async_copy(labels, marks, mark_sem),
    ]
    for copy in copies:
        copy.start()
    for node in range(nodes):
        part = pl.ds(node * segment, segment)
        copies.append(pltpu.make_async_copy(features.at[part], rows.at[part], row_sems.at[node]))
        copies[-1].start()
    copies[0].wait()
    me = lax.axis_index("rows")
    for node in range(nodes):
        owner = owner_list[node]
        apart = owner ^ me
        place = place_of(apart, owner, bits)
        section = 3 - 2 * (place >> (bits - 2)) - (apart & 1)
        listed[section * quarter + (place & (quarter - 1))] = node
    for copy in copies[1:]:
        copy.wait()
    fill(sent, 0, listed, rows, ids, marks, segment)


def first_sums(features, node_ids, labels, owners, bits):
    row_count, size = features.shape
    nodes = owners.shape[0]
    far = pl.BlockSpec(memory_space=pltpu.HBM)
    near = pl.BlockSpec(memory_space=pltpu.VMEM)
    words = pl.BlockSpec(memory_space=pltpu.SMEM)
    return pl.pallas_call(
        functools.partial(first_sums_kernel, bits),
        out_shape=(
            packed_shape(size, nodes // 4),
            pltpu.SMEM((nodes,), jnp.int32),
            pltpu.VMEM((row_count, size), jnp.bfloat16),
            pltpu.VMEM((row_count,), jnp.int32),
            pltpu.VMEM((row_count,), jnp.int32),
        ),
        in_specs=[far] * 4,
        out_specs=(near, words, near, near, near),
        scratch_shapes=[
            pltpu.SMEM((nodes,), jnp.int32),
            pltpu.SemaphoreType.DMA((nodes,)),
            pltpu.SemaphoreType.DMA,
            pltpu.SemaphoreType.DMA,
            pltpu.SemaphoreType.DMA,
        ],
        compiler_params=pltpu.CompilerParams(vmem_limit_bytes=32 << 20),
        name="first_sums",
    )(*(pltpu.with_memory_space_constraint(a, pltpu.HBM) for a in (owners, features, node_ids, labels)))


def more_sums_kernel(sections, listed, rows, ids, marks, *outs):
    segment = rows.shape[0] // listed.shape[0]
    for section, out in zip(sections, outs):
        fill(out, section, listed, rows, ids, marks, segment)


def more_sums(sections, listed, rows, ids, marks):
    row_count, size = rows.shape
    nodes = listed.shape[0]
    near = pl.BlockSpec(memory_space=pltpu.VMEM)
    return pl.pallas_call(
        functools.partial(more_sums_kernel, sections),
        out_shape=tuple(packed_shape(size, nodes // 4) for _ in sections),
        in_specs=[pl.BlockSpec(memory_space=pltpu.SMEM), near, near, near],
        out_specs=tuple(near for _ in sections),
        compiler_params=pltpu.CompilerParams(vmem_limit_bytes=32 << 20),
        cost_estimate=pl.CostEstimate(
            flops=row_count * size * size * len(sections) // 2, bytes_accessed=row_count * size, transcendentals=0
        ),
        name="more_sums",
    )(listed, rows, ids, marks)


def sweep(matrix, size):
    across = size // LANES
    lanes = lax.broadcasted_iota(jnp.int32, (1, size), 1)
    rows = lax.broadcasted_iota(jnp.int32, (PANEL, 1), 0)
    lane_id = lax.broadcasted_iota(jnp.int32, (PANEL, size), 1)
    row_id = lax.broadcasted_iota(jnp.int32, (PANEL, size), 0)
    odd = (lax.broadcasted_iota(jnp.int32, (PANEL, size), 0) & 1) == 1

    def spread(x, at):
        return jnp.broadcast_to(x[:, at : at + 1], (PANEL, LANES))

    def wide(x):
        return jnp.concatenate([x] * across, axis=1)

    panel = matrix[0:PANEL, :]
    for first in range(0, size, PANEL):
        last = first + PANEL
        inside = (lanes >= first) & (lanes < last)
        p1, p2, p3 = split(panel)
        left = jnp.concatenate([p1, p1, p2, p2, p1, p3], axis=0)
        column = [spread(panel, first + c) for c in range(PANEL)]
        if last < size:
            following = matrix[last : last + PANEL, :]
            ahead = [spread(following, first + c) for c in range(PANEL)]
        work = jnp.where(inside, jnp.where(lane_id == row_id + first, -1.0, 0.0), panel)
        own = jnp.zeros((PANEL, LANES), jnp.float32)
        cross = own
        for k in range(0, PANEL, 2):
            c0, c1 = column[k], column[k + 1]
            b00 = jnp.broadcast_to(c0[k : k + 1, :], (PANEL, LANES))
            b10 = jnp.broadcast_to(c0[k + 1 : k + 2, :], (PANEL, LANES))
            b11 = jnp.broadcast_to(c1[k + 1 : k + 2, :], (PANEL, LANES))
            inverse = 1.0 / (b00 * b11 - b10 * b10)
            n00, n10, n11 = b11 * inverse, -b10 * inverse, b00 * inverse
            pair = (rows == k) | (rows == k + 1)
            c0, c1 = jnp.where(pair, 0.0, c0), jnp.where(pair, 0.0, c1)
            f0, f1 = c0 * n00 + c1 * n10, c0 * n10 + c1 * n11
            own = jnp.where(rows == k, n00, jnp.where(rows == k + 1, n11, own))
            cross = jnp.where(pair, n10, cross)
            for c in range(k + 2, PANEL):
                column[c] = column[c] - f0 * column[c][k : k + 1, :] - f1 * column[c][k + 1 : k + 2, :]
            work = work - wide(f0) * work[k : k + 1, :] - wide(f1) * work[k + 1 : k + 2, :]
        other = jnp.where(odd, pltpu.roll(work, 1, 0), pltpu.roll(work, PANEL - 1, 0))
        work = work * wide(own) + other * wide(cross)
        if last < size:
            terms = [wide(ahead[c]) * work[c : c + 1, :] for c in range(PANEL)]
            while len(terms) > 1:
                terms = [terms[t] + terms[t + 1] for t in range(0, len(terms), 2)]
            panel = jnp.where(inside, 0.0, following) - terms[0]
        w1, w2, w3 = split(work)
        right = jnp.concatenate([w1, w2, w1, w2, w3, w1], axis=0)
        starts = list(range(0, size, LANES))
        needed = last + PANEL if last + PANEL < size else 0
        for base in sorted(starts, key=lambda t: not t <= needed < t + LANES):
            part = over_rows(left[:, base : base + LANES], right)
            matrix[base : base + LANES, :] = jnp.where(inside, 0.0, matrix[base : base + LANES, :]) - part
        matrix[first:last, :] = work


def solve_kernel(kept, came, planes, message, matrix):
    size = matrix.shape[0]
    half = size // 2
    packed = kept[0] + came[0]
    cross, mixed = packed[:half], packed[half:size]
    sums = jnp.concatenate([packed[size : size + CLASSES], packed[size + CLASSES : size + 2 * CLASSES]], axis=1)
    at = size + 2 * CLASSES
    diagonal, count_row = packed[at : at + 1], packed[at + 1 : at + 2]
    i = lax.broadcasted_iota(jnp.int32, (half, half), 0)
    j = lax.broadcasted_iota(jnp.int32, (half, half), 1)
    ci = lax.broadcasted_iota(jnp.int32, (CLASSES, half), 0)
    cj = lax.broadcasted_iota(jnp.int32, (CLASSES, half), 1)
    counts = jnp.sum(jnp.where(ci == cj, count_row, 0.0), axis=1, keepdims=True)
    total = jnp.sum(counts, axis=0, keepdims=True)
    centers = jnp.sum(sums, axis=0, keepdims=True) / total
    scaled = sums / jnp.maximum(counts, 1.0)
    shifts = (sums - counts * centers) / total
    between = wide_over_rows(sums, scaled)
    upper = jnp.where(i < j, mixed, 0.0)
    lower = jnp.where(i > j, mixed, 0.0)
    ridge = jnp.where(i == j, RIDGE, 0.0)
    start = upper + upper.T + jnp.where(i == j, mixed, 0.0)
    end = lower + lower.T + jnp.where(i == j, diagonal, 0.0)
    matrix[:half, :half] = (start - between[:half, :half]) / total + ridge
    matrix[:half, half:] = (cross - between[:half, half:]) / total
    matrix[half:, :half] = (cross.T - between[half:, :half]) / total
    matrix[half:, half:] = (end - between[half:, half:]) / total + ridge
    sweep(matrix, size)
    result = -jnp.dot(shifts, matrix[...], precision=HIGH, preferred_element_type=jnp.float32)
    planes[0] = result
    offsets = -jnp.sum(result * centers, axis=1, keepdims=True)
    lane = lax.broadcasted_iota(jnp.int32, (CLASSES, LANES), 1)
    parts = jnp.zeros((CLASSES, LANES), jnp.float32)
    for t, term in enumerate(split(offsets)):
        parts = jnp.where(lane == t, term.astype(jnp.float32), parts)
    message[0, :, :size] = result.astype(jnp.bfloat16)
    message[0, :, size:] = parts.astype(jnp.bfloat16)


def solve(kept, came, size):
    return pl.pallas_call(
        solve_kernel,
        out_shape=(
            jax.ShapeDtypeStruct((1, CLASSES, size), jnp.float32),
            jax.ShapeDtypeStruct((1, CLASSES, size + LANES), jnp.bfloat16),
        ),
        scratch_shapes=[pltpu.VMEM((size, size), jnp.float32)],
        compiler_params=pltpu.CompilerParams(vmem_limit_bytes=32 << 20),
        name="solve",
    )(kept, came)


def scores_kernel(bits, group, owners, features, node_ids, messages, scores):
    size = features.shape[1]
    segment = scores.shape[1] // group
    for g in range(group):
        node = pl.program_id(0) * group + g
        here = pl.ds(pl.multiple_of(node * segment, segment), segment)
        alive = node_ids[here].reshape(1, segment) == node
        owner = owners[node]
        apart = owner ^ lax.axis_index("rows")
        message = messages[place_of(apart, owner, bits) + ((apart & 1) << (bits - 1))]
        offsets = jnp.sum(message[:, size:].astype(jnp.float32), axis=1, keepdims=True)
        result = lax.dot_general(
            message[:, :size], features[here, :], (((1,), (1,)), ((), ())), preferred_element_type=jnp.float32
        )
        scores[:, g * segment : (g + 1) * segment] = jnp.where(alive, result + offsets, 0.0)


def all_scores(features, node_ids, owners, messages, bits):
    row_count, size = features.shape
    nodes = owners.shape[0]
    segment = row_count // nodes
    group = nodes // 2
    near = pl.BlockSpec(memory_space=pltpu.VMEM)
    return pl.pallas_call(
        functools.partial(scores_kernel, bits, group),
        out_shape=jax.ShapeDtypeStruct((CLASSES, row_count), jnp.float32),
        grid=(nodes // group,),
        in_specs=[pl.BlockSpec(memory_space=pltpu.SMEM), near, near, near],
        out_specs=pl.BlockSpec((CLASSES, segment * group), lambda n: (0, n)),
        compiler_params=pltpu.CompilerParams(vmem_limit_bytes=32 << 20),
        name="all_scores",
    )(owners, features, node_ids, messages)


def on_device(ranks, features, node_ids, labels, owners):
    size = features.shape[1]
    bits = ranks.bit_length() - 1
    orders = exchange_orders(bits)

    def swap(x, distances):
        return lax.ppermute(x, "rows", [(r, r ^ distances[r & 1]) for r in range(ranks)])

    def halving(x, step):
        return swap(x, [1 << order[step] for order in orders])

    sent, listed, rows, ids, marks = first_sums(features, node_ids, labels, owners, bits)
    came = swap(sent, (1, 1))
    (kept,) = more_sums((1,), listed, rows, ids, marks)
    sent = kept + came
    sent, later_list = lax.optimization_barrier((sent, listed))
    came = halving(sent, 0)
    sent, kept = more_sums((2, 3), later_list, rows, ids, marks)
    kept = (kept, swap(sent, (1, 1)))
    for step in range(1, bits - 1):
        middle = came.shape[0] // 2
        sent = sum(k[middle:] for k in kept) + came[middle:]
        next_came = halving(sent, step)
        kept = (sum(k[:middle] for k in kept) + came[:middle],)
        came = next_came
    planes, held = solve(kept[0], came, size)
    for step in reversed(range(bits - 1)):
        held = jnp.concatenate([held, halving(held, step)], axis=0)
    held = jnp.concatenate([held, swap(held, (1, 1))], axis=0)
    return planes, all_scores(rows, ids, owners, held, bits)


def solution(mesh):
    ranks = mesh.shape["rows"]
    in_specs = (P(("leaf", "rows"), None), P(("leaf", "rows")), P(("leaf", "rows")), P("leaf"))
    out_specs = (P(("leaf", "rows"), None, None), P(None, ("leaf", "rows")))
    return jax.shard_map(
        functools.partial(on_device, ranks), mesh=mesh, in_specs=in_specs, out_specs=out_specs, check_vma=False
    )
```

```python
import functools

import jax
import jax.numpy as jnp
from jax import lax
from jax.experimental import pallas as pl
from jax.experimental.pallas import tpu as pltpu
from jax.sharding import PartitionSpec as P

CLASSES = 16
RIDGE = 0.1
PANEL = 16
LANES = 128
HIGH = lax.Precision.HIGHEST


def split(x):
    hi = x.astype(jnp.bfloat16)
    rest = x - hi.astype(jnp.float32)
    mid = rest.astype(jnp.bfloat16)
    low = (rest - mid.astype(jnp.float32)).astype(jnp.bfloat16)
    return hi, mid, low


def over_rows(a, b):
    return lax.dot_general(a, b, (((0,), (0,)), ((), ())), preferred_element_type=jnp.float32)


def wide_over_rows(a, b):
    a1, a2, a3 = split(a)
    b1, b2, b3 = split(b)
    return over_rows(
        jnp.concatenate([a1, a1, a2, a2, a1, a3], axis=0), jnp.concatenate([b1, b2, b1, b2, b3, b1], axis=0)
    )


def exchange_orders(bits):
    plain = list(range(1, bits))
    return plain, plain if bits < 3 else [2, 1] + plain[2:]


def place_of(apart, owner, bits):
    even, odd = (
        sum(((apart >> b) & 1) << (bits - 2 - t) for t, b in enumerate(order)) for order in exchange_orders(bits)
    )
    return jnp.where((owner & 1) == 1, odd, even)


def packed_sums(x, alive, marks):
    segment, size = x.shape
    half = size // 2
    classes = lax.broadcasted_iota(jnp.int32, (CLASSES, segment), 0)
    hot = jnp.where((marks == classes) & alive, 1.0, 0.0)
    counts = jnp.sum(hot, axis=1, keepdims=True)
    live = jnp.where(alive, 1.0, 0.0).astype(jnp.bfloat16)
    left = jnp.concatenate([x.T * live, hot.astype(jnp.bfloat16)], axis=0)
    both = jnp.dot(left, x, preferred_element_type=jnp.float32)
    moment, sums = both[:size], both[size:]
    ci = lax.broadcasted_iota(jnp.int32, (CLASSES, half), 0)
    cj = lax.broadcasted_iota(jnp.int32, (CLASSES, half), 1)
    count_row = jnp.sum(jnp.where(ci == cj, counts, 0.0), axis=0, keepdims=True)
    i = lax.broadcasted_iota(jnp.int32, (half, half), 0)
    j = lax.broadcasted_iota(jnp.int32, (half, half), 1)
    last = moment[half:, half:]
    mixed = jnp.where(i <= j, moment[:half, :half], last)
    diagonal = jnp.sum(jnp.where(i == j, last, 0.0), axis=0, keepdims=True)
    ti = lax.broadcasted_iota(jnp.int32, (8, half), 0)
    tail = jnp.where(ti == 0, diagonal, jnp.where(ti == 1, count_row, 0.0))
    return moment[:half, half:], mixed, sums, tail


def packed_shape(size, blocks):
    return pltpu.VMEM((blocks, size + 2 * CLASSES + 8, size // 2), jnp.float32)


def fill(out, first, row_first, listed, rows, ids, marks, ready=None):
    size = rows.shape[2]
    segment = rows.shape[1]
    half = size // 2

    def step(q, carry):
        node = listed[first + q]
        if ready is not None:
            ready(first + q)
        here = pl.ds(pl.multiple_of(node * segment, segment), segment)
        alive = ids[here].reshape(1, segment) == node
        cross, mixed, sums, tail = packed_sums(rows[row_first + q], alive, marks[here].reshape(1, segment))
        out[q, 0:half] = cross
        out[q, half:size] = mixed
        out[q, size : size + CLASSES] = sums[:, :half]
        out[q, size + CLASSES : size + 2 * CLASSES] = sums[:, half:]
        out[q, size + 2 * CLASSES :] = tail
        return carry

    lax.fori_loop(0, out.shape[0], step, 0)


def row_copy(features, rows, sems, listed, first, position):
    segment = rows.shape[1]
    start = pl.multiple_of(listed[position] * segment, segment)
    slot = position - first
    return pltpu.make_async_copy(features.at[pl.ds(start, segment)], rows.at[slot], sems.at[slot])


def first_sums_kernel(
    bits, owners, features, node_ids, labels, sent, listed, rows, ids, marks, owner_list, row_sems, list_sem, id_sem, mark_sem
):
    nodes = owners.shape[0]
    blocks = sent.shape[0]
    copies = [
        pltpu.make_async_copy(owners, owner_list, list_sem),
        pltpu.make_async_copy(node_ids, ids, id_sem),
        pltpu.make_async_copy(labels, marks, mark_sem),
    ]
    for copy in copies:
        copy.start()
    copies[0].wait()
    me = lax.axis_index("rows")
    for node in range(nodes):
        owner = owner_list[node]
        apart = owner ^ me
        place = place_of(apart, owner, bits)
        chunk = 7 - 2 * (place >> (bits - 3)) - (apart & 1)
        listed[chunk * blocks + (place & (blocks - 1))] = node
    for position in range(nodes // 2):
        row_copy(features, rows, row_sems, listed, 0, position).start()
    for copy in copies[1:]:
        copy.wait()

    def ready(position):
        row_copy(features, rows, row_sems, listed, 0, position).wait()

    fill(sent, 0, 0, listed, rows, ids, marks, ready)
    for position in range(blocks, nodes // 2):
        ready(position)


def hbm(x):
    return pltpu.with_memory_space_constraint(x, pltpu.HBM)


def half_rows(features, nodes):
    row_count, size = features.shape
    return pltpu.VMEM((nodes // 2, row_count // nodes, size), features.dtype)


def first_sums(features, node_ids, labels, owners, bits):
    row_count, size = features.shape
    nodes = owners.shape[0]
    far = pl.BlockSpec(memory_space=pltpu.HBM)
    near = pl.BlockSpec(memory_space=pltpu.VMEM)
    words = pl.BlockSpec(memory_space=pltpu.SMEM)
    return pl.pallas_call(
        functools.partial(first_sums_kernel, bits),
        out_shape=(
            packed_shape(size, nodes // 8),
            pltpu.SMEM((nodes,), jnp.int32),
            half_rows(features, nodes),
            pltpu.VMEM((row_count,), jnp.int32),
            pltpu.VMEM((row_count,), jnp.int32),
        ),
        in_specs=[far] * 4,
        out_specs=(near, words, near, near, near),
        scratch_shapes=[
            pltpu.SMEM((nodes,), jnp.int32),
            pltpu.SemaphoreType.DMA((nodes // 2,)),
            pltpu.SemaphoreType.DMA,
            pltpu.SemaphoreType.DMA,
            pltpu.SemaphoreType.DMA,
        ],
        compiler_params=pltpu.CompilerParams(vmem_limit_bytes=32 << 20),
        name="first_sums",
    )(hbm(owners), hbm(features), hbm(node_ids), hbm(labels))


def loading_sums_kernel(listed, features, rows, ids, marks, early, late, later_rows, row_sems):
    nodes = listed.shape[0]
    blocks = early.shape[0]
    middle = nodes // 2
    for position in range(middle, nodes):
        row_copy(features, later_rows, row_sems, listed, middle, position).start()
    fill(early, 3 * blocks, 3 * blocks, listed, rows, ids, marks)

    def ready(position):
        row_copy(features, later_rows, row_sems, listed, middle, position).wait()

    fill(late, 4 * blocks, 0, listed, later_rows, ids, marks, ready)
    for position in range(middle + blocks, nodes):
        ready(position)


def loading_sums(features, listed, rows, ids, marks):
    size = features.shape[1]
    nodes = listed.shape[0]
    near = pl.BlockSpec(memory_space=pltpu.VMEM)
    return pl.pallas_call(
        loading_sums_kernel,
        out_shape=(packed_shape(size, nodes // 8),) * 2 + (half_rows(features, nodes),),
        in_specs=[pl.BlockSpec(memory_space=pltpu.SMEM), pl.BlockSpec(memory_space=pltpu.HBM), near, near, near],
        out_specs=(near, near, near),
        scratch_shapes=[pltpu.SemaphoreType.DMA((nodes // 2,))],
        compiler_params=pltpu.CompilerParams(vmem_limit_bytes=32 << 20),
        cost_estimate=sums_cost(features.shape, 2),
        name="loading_sums",
    )(listed, hbm(features), rows, ids, marks)


def sums_cost(shape, chunks):
    row_count, size = shape
    return pl.CostEstimate(
        flops=row_count * size * size * chunks // 4, bytes_accessed=row_count * size * chunks // 4, transcendentals=0
    )


def more_sums_kernel(chunks, listed, rows, ids, marks, *outs):
    for chunk, out in zip(chunks, outs):
        blocks = out.shape[0]
        fill(out, chunk * blocks, chunk * blocks % rows.shape[0], listed, rows, ids, marks)


def more_sums(chunks, listed, rows, ids, marks):
    size = rows.shape[2]
    nodes = listed.shape[0]
    near = pl.BlockSpec(memory_space=pltpu.VMEM)
    return pl.pallas_call(
        functools.partial(more_sums_kernel, chunks),
        out_shape=(packed_shape(size, nodes // 8),) * len(chunks),
        in_specs=[pl.BlockSpec(memory_space=pltpu.SMEM), near, near, near],
        out_specs=(near,) * len(chunks),
        compiler_params=pltpu.CompilerParams(vmem_limit_bytes=32 << 20),
        cost_estimate=sums_cost((ids.shape[0], size), len(chunks)),
        name="more_sums",
    )(listed, rows, ids, marks)


def sweep(matrix, size):
    across = size // LANES
    lanes = lax.broadcasted_iota(jnp.int32, (1, size), 1)
    rows = lax.broadcasted_iota(jnp.int32, (PANEL, 1), 0)
    lane_id = lax.broadcasted_iota(jnp.int32, (PANEL, size), 1)
    row_id = lax.broadcasted_iota(jnp.int32, (PANEL, size), 0)
    odd = (lax.broadcasted_iota(jnp.int32, (PANEL, size), 0) & 1) == 1

    def spread(x, at):
        return jnp.broadcast_to(x[:, at : at + 1], (PANEL, LANES))

    def wide(x):
        return jnp.concatenate([x] * across, axis=1)

    panel = matrix[0:PANEL, :]
    for first in range(0, size, PANEL):
        last = first + PANEL
        inside = (lanes >= first) & (lanes < last)
        p1, p2, p3 = split(panel)
        left = jnp.concatenate([p1, p1, p2, p2, p1, p3], axis=0)
        column = [spread(panel, first + c) for c in range(PANEL)]
        if last < size:
            following = matrix[last : last + PANEL, :]
            ahead = [spread(following, first + c) for c in range(PANEL)]
        work = jnp.where(inside, jnp.where(lane_id == row_id + first, -1.0, 0.0), panel)
        own = jnp.zeros((PANEL, LANES), jnp.float32)
        cross = own
        for k in range(0, PANEL, 2):
            c0, c1 = column[k], column[k + 1]
            b00 = jnp.broadcast_to(c0[k : k + 1, :], (PANEL, LANES))
            b10 = jnp.broadcast_to(c0[k + 1 : k + 2, :], (PANEL, LANES))
            b11 = jnp.broadcast_to(c1[k + 1 : k + 2, :], (PANEL, LANES))
            inverse = 1.0 / (b00 * b11 - b10 * b10)
            n00, n10, n11 = b11 * inverse, -b10 * inverse, b00 * inverse
            pair = (rows == k) | (rows == k + 1)
            c0, c1 = jnp.where(pair, 0.0, c0), jnp.where(pair, 0.0, c1)
            f0, f1 = c0 * n00 + c1 * n10, c0 * n10 + c1 * n11
            own = jnp.where(rows == k, n00, jnp.where(rows == k + 1, n11, own))
            cross = jnp.where(pair, n10, cross)
            for c in range(k + 2, PANEL):
                column[c] = column[c] - f0 * column[c][k : k + 1, :] - f1 * column[c][k + 1 : k + 2, :]
            work = work - wide(f0) * work[k : k + 1, :] - wide(f1) * work[k + 1 : k + 2, :]
        other = jnp.where(odd, pltpu.roll(work, 1, 0), pltpu.roll(work, PANEL - 1, 0))
        work = work * wide(own) + other * wide(cross)
        if last < size:
            terms = [wide(ahead[c]) * work[c : c + 1, :] for c in range(PANEL)]
            while len(terms) > 1:
                terms = [terms[t] + terms[t + 1] for t in range(0, len(terms), 2)]
            panel = jnp.where(inside, 0.0, following) - terms[0]
        w1, w2, w3 = split(work)
        right = jnp.concatenate([w1, w2, w1, w2, w3, w1], axis=0)
        starts = list(range(0, size, LANES))
        needed = last + PANEL if last + PANEL < size else 0
        for base in sorted(starts, key=lambda t: not t <= needed < t + LANES):
            part = over_rows(left[:, base : base + LANES], right)
            matrix[base : base + LANES, :] = jnp.where(inside, 0.0, matrix[base : base + LANES, :]) - part
        matrix[first:last, :] = work


def solve_kernel(kept, came, planes, message, matrix):
    size = matrix.shape[0]
    half = size // 2
    packed = kept[0] + came[0]
    cross, mixed = packed[:half], packed[half:size]
    sums = jnp.concatenate([packed[size : size + CLASSES], packed[size + CLASSES : size + 2 * CLASSES]], axis=1)
    at = size + 2 * CLASSES
    diagonal, count_row = packed[at : at + 1], packed[at + 1 : at + 2]
    i = lax.broadcasted_iota(jnp.int32, (half, half), 0)
    j = lax.broadcasted_iota(jnp.int32, (half, half), 1)
    ci = lax.broadcasted_iota(jnp.int32, (CLASSES, half), 0)
    cj = lax.broadcasted_iota(jnp.int32, (CLASSES, half), 1)
    counts = jnp.sum(jnp.where(ci == cj, count_row, 0.0), axis=1, keepdims=True)
    total = jnp.sum(counts, axis=0, keepdims=True)
    centers = jnp.sum(sums, axis=0, keepdims=True) / total
    scaled = sums / jnp.maximum(counts, 1.0)
    shifts = (sums - counts * centers) / total
    between = wide_over_rows(sums, scaled)
    upper = jnp.where(i < j, mixed, 0.0)
    lower = jnp.where(i > j, mixed, 0.0)
    ridge = jnp.where(i == j, RIDGE, 0.0)
    start = upper + upper.T + jnp.where(i == j, mixed, 0.0)
    end = lower + lower.T + jnp.where(i == j, diagonal, 0.0)
    matrix[:half, :half] = (start - between[:half, :half]) / total + ridge
    matrix[:half, half:] = (cross - between[:half, half:]) / total
    matrix[half:, :half] = (cross.T - between[half:, :half]) / total
    matrix[half:, half:] = (end - between[half:, half:]) / total + ridge
    sweep(matrix, size)
    result = -jnp.dot(shifts, matrix[...], precision=HIGH, preferred_element_type=jnp.float32)
    planes[0] = result
    offsets = -jnp.sum(result * centers, axis=1, keepdims=True)
    lane = lax.broadcasted_iota(jnp.int32, (CLASSES, LANES), 1)
    parts = jnp.zeros((CLASSES, LANES), jnp.float32)
    for t, term in enumerate(split(offsets)):
        parts = jnp.where(lane == t, term.astype(jnp.float32), parts)
    message[0, :, :size] = result.astype(jnp.bfloat16)
    message[0, :, size:] = parts.astype(jnp.bfloat16)


def solve(kept, came, size):
    return pl.pallas_call(
        solve_kernel,
        out_shape=(
            jax.ShapeDtypeStruct((1, CLASSES, size), jnp.float32),
            jax.ShapeDtypeStruct((1, CLASSES, size + LANES), jnp.bfloat16),
        ),
        scratch_shapes=[pltpu.VMEM((size, size), jnp.float32)],
        compiler_params=pltpu.CompilerParams(vmem_limit_bytes=32 << 20),
        name="solve",
    )(kept, came)


def scores_kernel(bits, group, owners, features, node_ids, messages, scores):
    size = features.shape[1]
    segment = scores.shape[1] // group
    for g in range(group):
        node = pl.program_id(0) * group + g
        here = pl.ds(pl.multiple_of(node * segment, segment), segment)
        alive = node_ids[here].reshape(1, segment) == node
        owner = owners[node]
        apart = owner ^ lax.axis_index("rows")
        message = messages[place_of(apart, owner, bits) + ((apart & 1) << (bits - 1))]
        offsets = jnp.sum(message[:, size:].astype(jnp.float32), axis=1, keepdims=True)
        result = lax.dot_general(
            message[:, :size], features[here, :], (((1,), (1,)), ((), ())), preferred_element_type=jnp.float32
        )
        scores[:, g * segment : (g + 1) * segment] = jnp.where(alive, result + offsets, 0.0)


def all_scores(features, node_ids, owners, messages, bits):
    row_count, size = features.shape
    nodes = owners.shape[0]
    segment = row_count // nodes
    group = nodes // 2
    near = pl.BlockSpec(memory_space=pltpu.VMEM)
    return pl.pallas_call(
        functools.partial(scores_kernel, bits, group),
        out_shape=jax.ShapeDtypeStruct((CLASSES, row_count), jnp.float32),
        grid=(nodes // group,),
        in_specs=[pl.BlockSpec(memory_space=pltpu.SMEM), near, near, near],
        out_specs=pl.BlockSpec((CLASSES, segment * group), lambda n: (0, n)),
        compiler_params=pltpu.CompilerParams(vmem_limit_bytes=32 << 20),
        name="all_scores",
    )(owners, features, node_ids, messages)


def on_device(ranks, features, node_ids, labels, owners):
    size = features.shape[1]
    bits = ranks.bit_length() - 1
    orders = exchange_orders(bits)

    def swap(x, distances):
        return lax.ppermute(x, "rows", [(r, r ^ distances[r & 1]) for r in range(ranks)])

    def halving(x, step):
        return swap(x, [1 << order[step] for order in orders])

    sent_a, listed, rows, ids, marks = first_sums(features, node_ids, labels, owners, bits)
    came_a = swap(sent_a, (1, 1))
    kept_a, sent_b = more_sums((1, 2), listed, rows, ids, marks)
    came_b = swap(sent_b, (1, 1))
    sent_a, listed = lax.optimization_barrier((kept_a + came_a, listed))
    came_a = halving(sent_a, 0)
    kept_b, next_a, rows_later = loading_sums(features, listed, rows, ids, marks)
    next_a = swap(next_a, (1, 1))
    sent_b, listed = lax.optimization_barrier((kept_b + came_b, listed))
    came_b = halving(sent_b, 0)
    (kept_a,) = more_sums((5,), listed, rows_later, ids, marks)
    sent_a, listed = lax.optimization_barrier((kept_a + next_a + came_a, listed))
    came = halving(sent_a, 1)
    next_b, kept_b = more_sums((6, 7), listed, rows_later, ids, marks)
    next_b = swap(next_b, (1, 1))
    kept = (kept_b, next_b, came_b)
    for step in range(2, bits - 1):
        middle = came.shape[0] // 2
        sent = sum(k[middle:] for k in kept) + came[middle:]
        next_came = halving(sent, step)
        kept = (sum(k[:middle] for k in kept) + came[:middle],)
        came = next_came
    planes, held = solve(kept[0], came, size)
    for step in reversed(range(bits - 1)):
        held = jnp.concatenate([held, halving(held, step)], axis=0)
    held = jnp.concatenate([held, swap(held, (1, 1))], axis=0)
    return planes, all_scores(features, ids, owners, held, bits)


def solution(mesh):
    ranks = mesh.shape["rows"]
    in_specs = (P(("leaf", "rows"), None), P(("leaf", "rows")), P(("leaf", "rows")), P("leaf"))
    out_specs = (P(("leaf", "rows"), None, None), P(None, ("leaf", "rows")))
    return jax.shard_map(
        functools.partial(on_device, ranks), mesh=mesh, in_specs=in_specs, out_specs=out_specs, check_vma=False
    )
```

```python
import functools

import jax
import jax.numpy as jnp
from jax import lax
from jax.experimental import pallas as pl
from jax.experimental.pallas import tpu as pltpu
from jax.sharding import PartitionSpec as P

CLASSES = 16
RIDGE = 0.1
PANEL = 16
LANES = 128
HIGH = lax.Precision.HIGHEST


def split(x):
    hi = x.astype(jnp.bfloat16)
    rest = x - hi.astype(jnp.float32)
    mid = rest.astype(jnp.bfloat16)
    low = (rest - mid.astype(jnp.float32)).astype(jnp.bfloat16)
    return hi, mid, low


def over_rows(a, b):
    return lax.dot_general(a, b, (((0,), (0,)), ((), ())), preferred_element_type=jnp.float32)


def wide_over_rows(a, b):
    a1, a2, a3 = split(a)
    b1, b2, b3 = split(b)
    return over_rows(
        jnp.concatenate([a1, a1, a2, a2, a1, a3], axis=0), jnp.concatenate([b1, b2, b1, b2, b3, b1], axis=0)
    )


def exchange_orders(bits):
    plain = list(range(1, bits))
    return plain, plain if bits < 3 else [2, 1] + plain[2:]


def place_of(apart, owner, bits):
    even, odd = (
        sum(((apart >> b) & 1) << (bits - 2 - t) for t, b in enumerate(order)) for order in exchange_orders(bits)
    )
    return jnp.where((owner & 1) == 1, odd, even)


def packed_sums(x, alive, marks):
    segment, size = x.shape
    half = size // 2
    classes = lax.broadcasted_iota(jnp.int32, (CLASSES, segment), 0)
    hot = jnp.where((marks == classes) & alive, 1.0, 0.0)
    counts = jnp.sum(hot, axis=1, keepdims=True)
    live = jnp.where(alive, 1.0, 0.0).astype(jnp.bfloat16)
    left = jnp.concatenate([x.T * live, hot.astype(jnp.bfloat16)], axis=0)
    both = jnp.dot(left, x, preferred_element_type=jnp.float32)
    moment, sums = both[:size], both[size:]
    ci = lax.broadcasted_iota(jnp.int32, (CLASSES, half), 0)
    cj = lax.broadcasted_iota(jnp.int32, (CLASSES, half), 1)
    count_row = jnp.sum(jnp.where(ci == cj, counts, 0.0), axis=0, keepdims=True)
    i = lax.broadcasted_iota(jnp.int32, (half, half), 0)
    j = lax.broadcasted_iota(jnp.int32, (half, half), 1)
    last = moment[half:, half:]
    mixed = jnp.where(i <= j, moment[:half, :half], last)
    diagonal = jnp.sum(jnp.where(i == j, last, 0.0), axis=0, keepdims=True)
    ti = lax.broadcasted_iota(jnp.int32, (8, half), 0)
    tail = jnp.where(ti == 0, diagonal, jnp.where(ti == 1, count_row, 0.0))
    return moment[:half, half:], mixed, sums, tail


def packed_shape(size, blocks):
    return pltpu.VMEM((blocks, size + 2 * CLASSES + 8, size // 2), jnp.float32)


def fill(out, first, listed, rows, ids, marks, ready=None):
    _, segment, size = rows.shape
    half = size // 2

    def step(q, carry):
        node = listed[first + q]
        if ready is not None:
            ready(node)
        here = pl.ds(pl.multiple_of(node * segment, segment), segment)
        alive = ids[here].reshape(1, segment) == node
        cross, mixed, sums, tail = packed_sums(rows[node], alive, marks[here].reshape(1, segment))
        out[q, 0:half] = cross
        out[q, half:size] = mixed
        out[q, size : size + CLASSES] = sums[:, :half]
        out[q, size + CLASSES : size + 2 * CLASSES] = sums[:, half:]
        out[q, size + 2 * CLASSES :] = tail
        return carry

    lax.fori_loop(0, out.shape[0], step, 0)


def first_sums_kernel(
    bits, owners, features, node_ids, labels, sent, listed, rows, ids, marks, owner_list, row_sems, list_sem, id_sem, mark_sem
):
    nodes = owners.shape[0]
    blocks = sent.shape[0]
    segment = rows.shape[1]
    copies = [
        pltpu.make_async_copy(owners, owner_list, list_sem),
        pltpu.make_async_copy(node_ids, ids, id_sem),
        pltpu.make_async_copy(labels, marks, mark_sem),
    ]
    for copy in copies:
        copy.start()

    def row_copy(node):
        start = pl.multiple_of(node * segment, segment)
        return pltpu.make_async_copy(features.at[pl.ds(start, segment)], rows.at[node], row_sems.at[node])

    for node in range(nodes):
        row_copy(node).start()
    copies[0].wait()
    me = lax.axis_index("rows")
    for node in range(nodes):
        owner = owner_list[node]
        apart = owner ^ me
        place = place_of(apart, owner, bits)
        chunk = 7 - 2 * (place >> (bits - 3)) - (apart & 1)
        listed[chunk * blocks + (place & (blocks - 1))] = node
    for copy in copies[1:]:
        copy.wait()
    fill(sent, 0, listed, rows, ids, marks, lambda node: row_copy(node).wait())
    for position in range(blocks, nodes):
        row_copy(listed[position]).wait()


def hbm(x):
    return pltpu.with_memory_space_constraint(x, pltpu.HBM)


def first_sums(features, node_ids, labels, owners, bits):
    row_count, size = features.shape
    nodes = owners.shape[0]
    far = pl.BlockSpec(memory_space=pltpu.HBM)
    near = pl.BlockSpec(memory_space=pltpu.VMEM)
    words = pl.BlockSpec(memory_space=pltpu.SMEM)
    return pl.pallas_call(
        functools.partial(first_sums_kernel, bits),
        out_shape=(
            packed_shape(size, nodes // 8),
            pltpu.SMEM((nodes,), jnp.int32),
            pltpu.VMEM((nodes, row_count // nodes, size), features.dtype),
            pltpu.VMEM((row_count,), jnp.int32),
            pltpu.VMEM((row_count,), jnp.int32),
        ),
        in_specs=[far] * 4,
        out_specs=(near, words, near, near, near),
        scratch_shapes=[
            pltpu.SMEM((nodes,), jnp.int32),
            pltpu.SemaphoreType.DMA((nodes,)),
            pltpu.SemaphoreType.DMA,
            pltpu.SemaphoreType.DMA,
            pltpu.SemaphoreType.DMA,
        ],
        compiler_params=pltpu.CompilerParams(vmem_limit_bytes=32 << 20),
        name="first_sums",
    )(hbm(owners), hbm(features), hbm(node_ids), hbm(labels))


def sums_cost(shape, chunks):
    row_count, size = shape
    return pl.CostEstimate(
        flops=row_count * size * size * chunks // 4, bytes_accessed=row_count * size * chunks // 4, transcendentals=0
    )


def more_sums_kernel(chunks, listed, rows, ids, marks, *outs):
    for chunk, out in zip(chunks, outs):
        blocks = out.shape[0]
        fill(out, chunk * blocks, listed, rows, ids, marks)


def more_sums(chunks, listed, rows, ids, marks):
    size = rows.shape[2]
    nodes = listed.shape[0]
    near = pl.BlockSpec(memory_space=pltpu.VMEM)
    return pl.pallas_call(
        functools.partial(more_sums_kernel, chunks),
        out_shape=(packed_shape(size, nodes // 8),) * len(chunks),
        in_specs=[pl.BlockSpec(memory_space=pltpu.SMEM), near, near, near],
        out_specs=(near,) * len(chunks),
        compiler_params=pltpu.CompilerParams(vmem_limit_bytes=32 << 20),
        cost_estimate=sums_cost((ids.shape[0], size), len(chunks)),
        name="more_sums",
    )(listed, rows, ids, marks)


def sweep(matrix, size):
    across = size // LANES
    lanes = lax.broadcasted_iota(jnp.int32, (1, size), 1)
    rows = lax.broadcasted_iota(jnp.int32, (PANEL, 1), 0)
    lane_id = lax.broadcasted_iota(jnp.int32, (PANEL, size), 1)
    row_id = lax.broadcasted_iota(jnp.int32, (PANEL, size), 0)
    odd = (lax.broadcasted_iota(jnp.int32, (PANEL, size), 0) & 1) == 1

    def spread(x, at):
        return jnp.broadcast_to(x[:, at : at + 1], (PANEL, LANES))

    def wide(x):
        return jnp.concatenate([x] * across, axis=1)

    panel = matrix[0:PANEL, :]
    for first in range(0, size, PANEL):
        last = first + PANEL
        inside = (lanes >= first) & (lanes < last)
        p1, p2, p3 = split(panel)
        left = jnp.concatenate([p1, p1, p2, p2, p1, p3], axis=0)
        column = [spread(panel, first + c) for c in range(PANEL)]
        if last < size:
            following = matrix[last : last + PANEL, :]
            ahead = [spread(following, first + c) for c in range(PANEL)]
        work = jnp.where(inside, jnp.where(lane_id == row_id + first, -1.0, 0.0), panel)
        own = jnp.zeros((PANEL, LANES), jnp.float32)
        cross = own
        for k in range(0, PANEL, 2):
            c0, c1 = column[k], column[k + 1]
            b00 = jnp.broadcast_to(c0[k : k + 1, :], (PANEL, LANES))
            b10 = jnp.broadcast_to(c0[k + 1 : k + 2, :], (PANEL, LANES))
            b11 = jnp.broadcast_to(c1[k + 1 : k + 2, :], (PANEL, LANES))
            inverse = 1.0 / (b00 * b11 - b10 * b10)
            n00, n10, n11 = b11 * inverse, -b10 * inverse, b00 * inverse
            pair = (rows == k) | (rows == k + 1)
            c0, c1 = jnp.where(pair, 0.0, c0), jnp.where(pair, 0.0, c1)
            f0, f1 = c0 * n00 + c1 * n10, c0 * n10 + c1 * n11
            own = jnp.where(rows == k, n00, jnp.where(rows == k + 1, n11, own))
            cross = jnp.where(pair, n10, cross)
            for c in range(k + 2, PANEL):
                column[c] = column[c] - f0 * column[c][k : k + 1, :] - f1 * column[c][k + 1 : k + 2, :]
            work = work - wide(f0) * work[k : k + 1, :] - wide(f1) * work[k + 1 : k + 2, :]
        other = jnp.where(odd, pltpu.roll(work, 1, 0), pltpu.roll(work, PANEL - 1, 0))
        work = work * wide(own) + other * wide(cross)
        if last < size:
            terms = [wide(ahead[c]) * work[c : c + 1, :] for c in range(PANEL)]
            while len(terms) > 1:
                terms = [terms[t] + terms[t + 1] for t in range(0, len(terms), 2)]
            panel = jnp.where(inside, 0.0, following) - terms[0]
        w1, w2, w3 = split(work)
        right = jnp.concatenate([w1, w2, w1, w2, w3, w1], axis=0)
        starts = list(range(0, size, LANES))
        needed = last + PANEL if last + PANEL < size else 0
        for base in sorted(starts, key=lambda t: not t <= needed < t + LANES):
            part = over_rows(left[:, base : base + LANES], right)
            matrix[base : base + LANES, :] = jnp.where(inside, 0.0, matrix[base : base + LANES, :]) - part
        matrix[first:last, :] = work


def solve_kernel(kept, came, planes, message, matrix):
    size = matrix.shape[0]
    half = size // 2
    packed = kept[0] + came[0]
    cross, mixed = packed[:half], packed[half:size]
    sums = jnp.concatenate([packed[size : size + CLASSES], packed[size + CLASSES : size + 2 * CLASSES]], axis=1)
    at = size + 2 * CLASSES
    diagonal, count_row = packed[at : at + 1], packed[at + 1 : at + 2]
    i = lax.broadcasted_iota(jnp.int32, (half, half), 0)
    j = lax.broadcasted_iota(jnp.int32, (half, half), 1)
    ci = lax.broadcasted_iota(jnp.int32, (CLASSES, half), 0)
    cj = lax.broadcasted_iota(jnp.int32, (CLASSES, half), 1)
    counts = jnp.sum(jnp.where(ci == cj, count_row, 0.0), axis=1, keepdims=True)
    total = jnp.sum(counts, axis=0, keepdims=True)
    centers = jnp.sum(sums, axis=0, keepdims=True) / total
    scaled = sums / jnp.maximum(counts, 1.0)
    shifts = (sums - counts * centers) / total
    between = wide_over_rows(sums, scaled)
    upper = jnp.where(i < j, mixed, 0.0)
    lower = jnp.where(i > j, mixed, 0.0)
    ridge = jnp.where(i == j, RIDGE, 0.0)
    start = upper + upper.T + jnp.where(i == j, mixed, 0.0)
    end = lower + lower.T + jnp.where(i == j, diagonal, 0.0)
    matrix[:half, :half] = (start - between[:half, :half]) / total + ridge
    matrix[:half, half:] = (cross - between[:half, half:]) / total
    matrix[half:, :half] = (cross.T - between[half:, :half]) / total
    matrix[half:, half:] = (end - between[half:, half:]) / total + ridge
    sweep(matrix, size)
    result = -jnp.dot(shifts, matrix[...], precision=HIGH, preferred_element_type=jnp.float32)
    planes[0] = result
    offsets = -jnp.sum(result * centers, axis=1, keepdims=True)
    lane = lax.broadcasted_iota(jnp.int32, (CLASSES, LANES), 1)
    parts = jnp.zeros((CLASSES, LANES), jnp.float32)
    for t, term in enumerate(split(offsets)):
        parts = jnp.where(lane == t, term.astype(jnp.float32), parts)
    message[0, :, :size] = result.astype(jnp.bfloat16)
    message[0, :, size:] = parts.astype(jnp.bfloat16)


def solve(kept, came, size):
    return pl.pallas_call(
        solve_kernel,
        out_shape=(
            jax.ShapeDtypeStruct((1, CLASSES, size), jnp.float32),
            jax.ShapeDtypeStruct((1, CLASSES, size + LANES), jnp.bfloat16),
        ),
        scratch_shapes=[pltpu.VMEM((size, size), jnp.float32)],
        compiler_params=pltpu.CompilerParams(vmem_limit_bytes=32 << 20),
        name="solve",
    )(kept, came)


def scores_kernel(parity, listed, rows, ids, messages, *refs):
    scores, scratch, sems = refs[-3:]
    nodes, segment, size = rows.shape
    blocks = nodes // 8
    copies = []
    for chunk in range(1 - parity, 8, 2):
        for q in range(blocks):
            node = listed[chunk * blocks + q]
            start = pl.multiple_of(node * segment, segment)
            alive = ids[pl.ds(start, segment)].reshape(1, segment) == node
            message = messages[(7 - chunk) // 2 * blocks + q]
            offsets = jnp.sum(message[:, size:].astype(jnp.float32), axis=1, keepdims=True)
            result = lax.dot_general(
                message[:, :size], rows[node], (((1,), (1,)), ((), ())), preferred_element_type=jnp.float32
            )
            slot = len(copies)
            scratch[slot] = jnp.where(alive, result + offsets, 0.0)
            copies.append(
                pltpu.make_async_copy(scratch.at[slot], scores.at[:, pl.ds(start, segment)], sems.at[slot])
            )
            copies[-1].start()
    for copy in copies:
        copy.wait()


def half_scores(parity, listed, rows, ids, messages, *earlier):
    nodes, segment, _ = rows.shape
    near = pl.BlockSpec(memory_space=pltpu.VMEM)
    far = pl.BlockSpec(memory_space=pltpu.HBM)
    return pl.pallas_call(
        functools.partial(scores_kernel, parity),
        out_shape=pltpu.HBM((CLASSES, nodes * segment), jnp.float32),
        in_specs=[pl.BlockSpec(memory_space=pltpu.SMEM), near, near, near] + [far] * len(earlier),
        out_specs=far,
        scratch_shapes=[
            pltpu.VMEM((nodes // 2, CLASSES, segment), jnp.float32),
            pltpu.SemaphoreType.DMA((nodes // 2,)),
        ],
        input_output_aliases={4: 0} if earlier else {},
        compiler_params=pltpu.CompilerParams(vmem_limit_bytes=32 << 20),
        name="half_scores",
    )(listed, rows, ids, messages, *(hbm(e) for e in earlier))


def on_device(ranks, features, node_ids, labels, owners):
    size = features.shape[1]
    bits = ranks.bit_length() - 1
    orders = exchange_orders(bits)

    def swap(x, distances):
        return lax.ppermute(x, "rows", [(r, r ^ distances[r & 1]) for r in range(ranks)])

    def halving(x, step):
        return swap(x, [1 << order[step] for order in orders])

    sent_a, listed, rows, ids, marks = first_sums(features, node_ids, labels, owners, bits)
    came_a = swap(sent_a, (1, 1))
    kept_a, sent_b = more_sums((1, 2), listed, rows, ids, marks)
    came_b = swap(sent_b, (1, 1))
    sent_a, listed = lax.optimization_barrier((kept_a + came_a, listed))
    came_a = halving(sent_a, 0)
    kept_b, next_a = more_sums((3, 4), listed, rows, ids, marks)
    next_a = swap(next_a, (1, 1))
    sent_b, listed = lax.optimization_barrier((kept_b + came_b, listed))
    came_b = halving(sent_b, 0)
    (kept_a,) = more_sums((5,), listed, rows, ids, marks)
    sent_a, listed = lax.optimization_barrier((kept_a + next_a + came_a, listed))
    came = halving(sent_a, 1)
    next_b, kept_b = more_sums((6, 7), listed, rows, ids, marks)
    next_b = swap(next_b, (1, 1))
    kept = (kept_b, next_b, came_b)
    for step in range(2, bits - 1):
        middle = came.shape[0] // 2
        sent = sum(k[middle:] for k in kept) + came[middle:]
        next_came = halving(sent, step)
        kept = (sum(k[:middle] for k in kept) + came[:middle],)
        came = next_came
    planes, held = solve(kept[0], came, size)
    for step in reversed(range(bits - 1)):
        held = jnp.concatenate([held, halving(held, step)], axis=0)
    others = swap(held, (1, 1))
    scores = half_scores(0, listed, rows, ids, held)
    return planes, half_scores(1, listed, rows, ids, others, scores)


def solution(mesh):
    ranks = mesh.shape["rows"]
    in_specs = (P(("leaf", "rows"), None), P(("leaf", "rows")), P(("leaf", "rows")), P("leaf"))
    out_specs = (P(("leaf", "rows"), None, None), P(None, ("leaf", "rows")))
    return jax.shard_map(
        functools.partial(on_device, ranks), mesh=mesh, in_specs=in_specs, out_specs=out_specs, check_vma=False
    )
```

```python
import functools

import jax
import jax.numpy as jnp
from jax import lax
from jax.experimental import pallas as pl
from jax.experimental.pallas import tpu as pltpu
from jax.sharding import PartitionSpec as P

CLASSES = 16
RIDGE = 0.1
PANEL = 16
LANES = 128
HIGH = lax.Precision.HIGHEST


def split(x):
    hi = x.astype(jnp.bfloat16)
    rest = x - hi.astype(jnp.float32)
    mid = rest.astype(jnp.bfloat16)
    low = (rest - mid.astype(jnp.float32)).astype(jnp.bfloat16)
    return hi, mid, low


def over_rows(a, b):
    return lax.dot_general(a, b, (((0,), (0,)), ((), ())), preferred_element_type=jnp.float32)


def wide_over_rows(a, b):
    a1, a2, a3 = split(a)
    b1, b2, b3 = split(b)
    return over_rows(
        jnp.concatenate([a1, a1, a2, a2, a1, a3], axis=0), jnp.concatenate([b1, b2, b1, b2, b3, b1], axis=0)
    )


def exchange_orders(bits):
    plain = list(range(1, bits))
    return plain, plain if bits < 3 else [2, 1] + plain[2:]


def place_of(apart, owner, bits):
    even, odd = (
        sum(((apart >> b) & 1) << (bits - 2 - t) for t, b in enumerate(order)) for order in exchange_orders(bits)
    )
    return jnp.where((owner & 1) == 1, odd, even)


def packed_sums(x, alive, marks):
    segment, size = x.shape
    half = size // 2
    classes = lax.broadcasted_iota(jnp.int32, (CLASSES, segment), 0)
    hot = jnp.where((marks == classes) & alive, 1.0, 0.0)
    counts = jnp.sum(hot, axis=1, keepdims=True)
    live = jnp.where(alive, 1.0, 0.0).astype(jnp.bfloat16)
    left = jnp.concatenate([x.T * live, hot.astype(jnp.bfloat16)], axis=0)
    both = jnp.dot(left, x, preferred_element_type=jnp.float32)
    moment, sums = both[:size], both[size:]
    ci = lax.broadcasted_iota(jnp.int32, (CLASSES, half), 0)
    cj = lax.broadcasted_iota(jnp.int32, (CLASSES, half), 1)
    count_row = jnp.sum(jnp.where(ci == cj, counts, 0.0), axis=0, keepdims=True)
    i = lax.broadcasted_iota(jnp.int32, (half, half), 0)
    j = lax.broadcasted_iota(jnp.int32, (half, half), 1)
    last = moment[half:, half:]
    mixed = jnp.where(i <= j, moment[:half, :half], last)
    diagonal = jnp.sum(jnp.where(i == j, last, 0.0), axis=0, keepdims=True)
    ti = lax.broadcasted_iota(jnp.int32, (8, half), 0)
    tail = jnp.where(ti == 0, diagonal, jnp.where(ti == 1, count_row, 0.0))
    return moment[:half, half:], mixed, sums, tail


def packed_shape(size, blocks):
    return pltpu.VMEM((blocks, size + 2 * CLASSES + 8, size // 2), jnp.float32)


def fill(out, first, listed, rows, ids, marks, ready=None):
    _, segment, size = rows.shape
    half = size // 2

    def step(q, carry):
        node = listed[first + q]
        if ready is not None:
            ready(node)
        here = pl.ds(pl.multiple_of(node * segment, segment), segment)
        alive = ids[here].reshape(1, segment) == node
        cross, mixed, sums, tail = packed_sums(rows[node], alive, marks[here].reshape(1, segment))
        out[q, 0:half] = cross
        out[q, half:size] = mixed
        out[q, size : size + CLASSES] = sums[:, :half]
        out[q, size + CLASSES : size + 2 * CLASSES] = sums[:, half:]
        out[q, size + 2 * CLASSES :] = tail
        return carry

    lax.fori_loop(0, out.shape[0], step, 0)


def first_sums_kernel(
    bits, owners, features, node_ids, labels, sent, listed, rows, ids, marks, owner_list, row_sems, list_sem, id_sem, mark_sem
):
    nodes = owners.shape[0]
    blocks = sent.shape[0]
    segment = rows.shape[1]
    copies = [
        pltpu.make_async_copy(owners, owner_list, list_sem),
        pltpu.make_async_copy(node_ids, ids, id_sem),
        pltpu.make_async_copy(labels, marks, mark_sem),
    ]
    for copy in copies:
        copy.start()

    def row_copy(node):
        start = pl.multiple_of(node * segment, segment)
        return pltpu.make_async_copy(features.at[pl.ds(start, segment)], rows.at[node], row_sems.at[node])

    for node in range(nodes):
        row_copy(node).start()
    copies[0].wait()
    me = lax.axis_index("rows")
    for node in range(nodes):
        owner = owner_list[node]
        apart = owner ^ me
        place = place_of(apart, owner, bits)
        chunk = 7 - 2 * (place >> (bits - 3)) - (apart & 1)
        listed[chunk * blocks + (place & (blocks - 1))] = node
    for copy in copies[1:]:
        copy.wait()
    fill(sent, 0, listed, rows, ids, marks, lambda node: row_copy(node).wait())
    for position in range(blocks, nodes):
        row_copy(listed[position]).wait()


def hbm(x):
    return pltpu.with_memory_space_constraint(x, pltpu.HBM)


def first_sums(features, node_ids, labels, owners, bits):
    row_count, size = features.shape
    nodes = owners.shape[0]
    far = pl.BlockSpec(memory_space=pltpu.HBM)
    near = pl.BlockSpec(memory_space=pltpu.VMEM)
    words = pl.BlockSpec(memory_space=pltpu.SMEM)
    return pl.pallas_call(
        functools.partial(first_sums_kernel, bits),
        out_shape=(
            packed_shape(size, nodes // 8),
            pltpu.SMEM((nodes,), jnp.int32),
            pltpu.VMEM((nodes, row_count // nodes, size), features.dtype),
            pltpu.VMEM((row_count,), jnp.int32),
            pltpu.VMEM((row_count,), jnp.int32),
        ),
        in_specs=[far] * 4,
        out_specs=(near, words, near, near, near),
        scratch_shapes=[
            pltpu.SMEM((nodes,), jnp.int32),
            pltpu.SemaphoreType.DMA((nodes,)),
            pltpu.SemaphoreType.DMA,
            pltpu.SemaphoreType.DMA,
            pltpu.SemaphoreType.DMA,
        ],
        compiler_params=pltpu.CompilerParams(vmem_limit_bytes=32 << 20),
        name="first_sums",
    )(hbm(owners), hbm(features), hbm(node_ids), hbm(labels))


def sums_cost(shape, chunks):
    row_count, size = shape
    return pl.CostEstimate(
        flops=row_count * size * size * chunks // 4, bytes_accessed=row_count * size * chunks // 4, transcendentals=0
    )


def more_sums_kernel(chunks, listed, rows, ids, marks, *outs):
    for chunk, out in zip(chunks, outs):
        blocks = out.shape[0]
        fill(out, chunk * blocks, listed, rows, ids, marks)


def more_sums(chunks, listed, rows, ids, marks):
    size = rows.shape[2]
    nodes = listed.shape[0]
    near = pl.BlockSpec(memory_space=pltpu.VMEM)
    return pl.pallas_call(
        functools.partial(more_sums_kernel, chunks),
        out_shape=(packed_shape(size, nodes // 8),) * len(chunks),
        in_specs=[pl.BlockSpec(memory_space=pltpu.SMEM), near, near, near],
        out_specs=(near,) * len(chunks),
        compiler_params=pltpu.CompilerParams(vmem_limit_bytes=32 << 20),
        cost_estimate=sums_cost((ids.shape[0], size), len(chunks)),
        name="more_sums",
    )(listed, rows, ids, marks)


def sweep(matrix, size, columns, works):
    across = size // LANES
    lanes = lax.broadcasted_iota(jnp.int32, (1, size), 1)
    rows = lax.broadcasted_iota(jnp.int32, (PANEL, 1), 0)
    lane_id = lax.broadcasted_iota(jnp.int32, (PANEL, size), 1)
    row_id = lax.broadcasted_iota(jnp.int32, (PANEL, size), 0)
    odd = (lax.broadcasted_iota(jnp.int32, (PANEL, size), 0) & 1) == 1

    def spread(x, at):
        return jnp.broadcast_to(x[:, at : at + 1], (PANEL, LANES))

    def wide(x):
        return jnp.concatenate([x] * across, axis=1)

    panel = matrix[0:PANEL, :]
    for first in range(0, size, PANEL):
        last = first + PANEL
        inside = (lanes >= first) & (lanes < last)
        p1, p2, p3 = split(panel)
        left = jnp.concatenate([p1, p1, p2, p2, p1, p3], axis=0)
        column = [spread(panel, first + c) for c in range(PANEL)]
        if last < size:
            following = matrix[last : last + PANEL, :]
            ahead = [spread(following, first + c) for c in range(PANEL)]
        work = jnp.where(inside, jnp.where(lane_id == row_id + first, -1.0, 0.0), panel)
        own = jnp.zeros((PANEL, LANES), jnp.float32)
        cross = own
        for k in range(0, PANEL, 2):
            c0, c1 = column[k], column[k + 1]
            group, turn = k // 8 * 8, k // 2 % 2
            for c in range(k + 2, PANEL):
                columns[turn, c, 0:8] = column[c][group : group + 8, :]
            works[turn, 0:8] = work[group : group + 8, :]

            def repeated(ref, at, group=group):
                rows8 = ref[pl.ds(at - group, 8, stride=0), :]
                return jnp.concatenate([rows8] * (PANEL // 8), axis=0)

            b00 = jnp.broadcast_to(c0[k : k + 1, :], (PANEL, LANES))
            b10 = jnp.broadcast_to(c0[k + 1 : k + 2, :], (PANEL, LANES))
            b11 = jnp.broadcast_to(c1[k + 1 : k + 2, :], (PANEL, LANES))
            inverse = 1.0 / (b00 * b11 - b10 * b10)
            n00, n10, n11 = b11 * inverse, -b10 * inverse, b00 * inverse
            pair = (rows == k) | (rows == k + 1)
            c0, c1 = jnp.where(pair, 0.0, c0), jnp.where(pair, 0.0, c1)
            f0, f1 = c0 * n00 + c1 * n10, c0 * n10 + c1 * n11
            own = jnp.where(rows == k, n00, jnp.where(rows == k + 1, n11, own))
            cross = jnp.where(pair, n10, cross)
            for c in range(k + 2, PANEL):
                row0, row1 = (repeated(columns.at[turn, c], k + t) for t in range(2))
                column[c] = column[c] - f0 * row0 - f1 * row1
            row0, row1 = (repeated(works.at[turn], k + t) for t in range(2))
            work = work - wide(f0) * row0 - wide(f1) * row1
        other = jnp.where(odd, pltpu.roll(work, 1, 0), pltpu.roll(work, PANEL - 1, 0))
        work = work * wide(own) + other * wide(cross)
        if last < size:
            terms = [wide(ahead[c]) * work[c : c + 1, :] for c in range(PANEL)]
            while len(terms) > 1:
                terms = [terms[t] + terms[t + 1] for t in range(0, len(terms), 2)]
            panel = jnp.where(inside, 0.0, following) - terms[0]
        w1, w2, w3 = split(work)
        right = jnp.concatenate([w1, w2, w1, w2, w3, w1], axis=0)
        starts = list(range(0, size, LANES))
        needed = last + PANEL if last + PANEL < size else 0
        for base in sorted(starts, key=lambda t: not t <= needed < t + LANES):
            part = over_rows(left[:, base : base + LANES], right)
            matrix[base : base + LANES, :] = jnp.where(inside, 0.0, matrix[base : base + LANES, :]) - part
        matrix[first:last, :] = work


def solve_kernel(kept, came, planes, message, matrix, columns, works):
    size = matrix.shape[0]
    half = size // 2
    packed = kept[0] + came[0]
    cross, mixed = packed[:half], packed[half:size]
    sums = jnp.concatenate([packed[size : size + CLASSES], packed[size + CLASSES : size + 2 * CLASSES]], axis=1)
    at = size + 2 * CLASSES
    diagonal, count_row = packed[at : at + 1], packed[at + 1 : at + 2]
    i = lax.broadcasted_iota(jnp.int32, (half, half), 0)
    j = lax.broadcasted_iota(jnp.int32, (half, half), 1)
    ci = lax.broadcasted_iota(jnp.int32, (CLASSES, half), 0)
    cj = lax.broadcasted_iota(jnp.int32, (CLASSES, half), 1)
    counts = jnp.sum(jnp.where(ci == cj, count_row, 0.0), axis=1, keepdims=True)
    total = jnp.sum(counts, axis=0, keepdims=True)
    centers = jnp.sum(sums, axis=0, keepdims=True) / total
    scaled = sums / jnp.maximum(counts, 1.0)
    shifts = (sums - counts * centers) / total
    between = wide_over_rows(sums, scaled)
    upper = jnp.where(i < j, mixed, 0.0)
    lower = jnp.where(i > j, mixed, 0.0)
    ridge = jnp.where(i == j, RIDGE, 0.0)
    start = upper + upper.T + jnp.where(i == j, mixed, 0.0)
    end = lower + lower.T + jnp.where(i == j, diagonal, 0.0)
    matrix[:half, :half] = (start - between[:half, :half]) / total + ridge
    matrix[:half, half:] = (cross - between[:half, half:]) / total
    matrix[half:, :half] = (cross.T - between[half:, :half]) / total
    matrix[half:, half:] = (end - between[half:, half:]) / total + ridge
    sweep(matrix, size, columns, works)
    result = -jnp.dot(shifts, matrix[...], precision=HIGH, preferred_element_type=jnp.float32)
    planes[0] = result
    offsets = -jnp.sum(result * centers, axis=1, keepdims=True)
    lane = lax.broadcasted_iota(jnp.int32, (CLASSES, LANES), 1)
    parts = jnp.zeros((CLASSES, LANES), jnp.float32)
    for t, term in enumerate(split(offsets)):
        parts = jnp.where(lane == t, term.astype(jnp.float32), parts)
    message[0, :, :size] = result.astype(jnp.bfloat16)
    message[0, :, size:] = parts.astype(jnp.bfloat16)


def solve(kept, came, size):
    return pl.pallas_call(
        solve_kernel,
        out_shape=(
            jax.ShapeDtypeStruct((1, CLASSES, size), jnp.float32),
            jax.ShapeDtypeStruct((1, CLASSES, size + LANES), jnp.bfloat16),
        ),
        scratch_shapes=[
            pltpu.VMEM((size, size), jnp.float32),
            pltpu.VMEM((2, PANEL, 16, LANES), jnp.float32),
            pltpu.VMEM((2, 16, size), jnp.float32),
        ],
        compiler_params=pltpu.CompilerParams(vmem_limit_bytes=32 << 20),
        name="solve",
    )(kept, came)


def scores_kernel(parity, listed, rows, ids, messages, *refs):
    scores, scratch, sems = refs[-3:]
    nodes, segment, size = rows.shape
    blocks = nodes // 8
    copies = []
    for chunk in range(1 - parity, 8, 2):
        for q in range(blocks):
            node = listed[chunk * blocks + q]
            start = pl.multiple_of(node * segment, segment)
            alive = ids[pl.ds(start, segment)].reshape(1, segment) == node
            message = messages[(7 - chunk) // 2 * blocks + q]
            offsets = jnp.sum(message[:, size:].astype(jnp.float32), axis=1, keepdims=True)
            result = lax.dot_general(
                message[:, :size], rows[node], (((1,), (1,)), ((), ())), preferred_element_type=jnp.float32
            )
            slot = len(copies)
            scratch[slot] = jnp.where(alive, result + offsets, 0.0)
            copies.append(
                pltpu.make_async_copy(scratch.at[slot], scores.at[:, pl.ds(start, segment)], sems.at[slot])
            )
            copies[-1].start()
    for copy in copies:
        copy.wait()


def half_scores(parity, listed, rows, ids, messages, *earlier):
    nodes, segment, _ = rows.shape
    near = pl.BlockSpec(memory_space=pltpu.VMEM)
    far = pl.BlockSpec(memory_space=pltpu.HBM)
    return pl.pallas_call(
        functools.partial(scores_kernel, parity),
        out_shape=pltpu.HBM((CLASSES, nodes * segment), jnp.float32),
        in_specs=[pl.BlockSpec(memory_space=pltpu.SMEM), near, near, near] + [far] * len(earlier),
        out_specs=far,
        scratch_shapes=[
            pltpu.VMEM((nodes // 2, CLASSES, segment), jnp.float32),
            pltpu.SemaphoreType.DMA((nodes // 2,)),
        ],
        input_output_aliases={4: 0} if earlier else {},
        compiler_params=pltpu.CompilerParams(vmem_limit_bytes=32 << 20),
        name="half_scores",
    )(listed, rows, ids, messages, *(hbm(e) for e in earlier))


def on_device(ranks, features, node_ids, labels, owners):
    size = features.shape[1]
    bits = ranks.bit_length() - 1
    orders = exchange_orders(bits)

    def swap(x, distances):
        return lax.ppermute(x, "rows", [(r, r ^ distances[r & 1]) for r in range(ranks)])

    def halving(x, step):
        return swap(x, [1 << order[step] for order in orders])

    sent_a, listed, rows, ids, marks = first_sums(features, node_ids, labels, owners, bits)
    came_a = swap(sent_a, (1, 1))
    kept_a, sent_b = more_sums((1, 2), listed, rows, ids, marks)
    came_b = swap(sent_b, (1, 1))
    sent_a, listed = lax.optimization_barrier((kept_a + came_a, listed))
    came_a = halving(sent_a, 0)
    kept_b, next_a = more_sums((3, 4), listed, rows, ids, marks)
    next_a = swap(next_a, (1, 1))
    sent_b, listed = lax.optimization_barrier((kept_b + came_b, listed))
    came_b = halving(sent_b, 0)
    (kept_a,) = more_sums((5,), listed, rows, ids, marks)
    sent_a, listed = lax.optimization_barrier((kept_a + next_a + came_a, listed))
    came = halving(sent_a, 1)
    next_b, kept_b = more_sums((6, 7), listed, rows, ids, marks)
    next_b = swap(next_b, (1, 1))
    kept = (kept_b, next_b, came_b)
    for step in range(2, bits - 1):
        middle = came.shape[0] // 2
        sent = sum(k[middle:] for k in kept) + came[middle:]
        next_came = halving(sent, step)
        kept = (sum(k[:middle] for k in kept) + came[:middle],)
        came = next_came
    planes, held = solve(kept[0], came, size)
    for step in reversed(range(bits - 1)):
        held = jnp.concatenate([held, halving(held, step)], axis=0)
    others = swap(held, (1, 1))
    scores = half_scores(0, listed, rows, ids, held)
    return planes, half_scores(1, listed, rows, ids, others, scores)


def solution(mesh):
    ranks = mesh.shape["rows"]
    in_specs = (P(("leaf", "rows"), None), P(("leaf", "rows")), P(("leaf", "rows")), P("leaf"))
    out_specs = (P(("leaf", "rows"), None, None), P(None, ("leaf", "rows")))
    return jax.shard_map(
        functools.partial(on_device, ranks), mesh=mesh, in_specs=in_specs, out_specs=out_specs, check_vma=False
    )
```

```python
import functools

import jax
import jax.numpy as jnp
from jax import lax
from jax.experimental import pallas as pl
from jax.experimental.pallas import tpu as pltpu
from jax.sharding import PartitionSpec as P

CLASSES = 16
RIDGE = 0.1
PANEL = 16
LANES = 128
HIGH = lax.Precision.HIGHEST


def split(x):
    hi = x.astype(jnp.bfloat16)
    rest = x - hi.astype(jnp.float32)
    mid = rest.astype(jnp.bfloat16)
    low = (rest - mid.astype(jnp.float32)).astype(jnp.bfloat16)
    return hi, mid, low


def over_rows(a, b):
    return lax.dot_general(a, b, (((0,), (0,)), ((), ())), preferred_element_type=jnp.float32)


def wide_over_rows(a, b):
    a1, a2, a3 = split(a)
    b1, b2, b3 = split(b)
    return over_rows(
        jnp.concatenate([a1, a1, a2, a2, a1, a3], axis=0), jnp.concatenate([b1, b2, b1, b2, b3, b1], axis=0)
    )


def exchange_orders(bits):
    plain = list(range(1, bits))
    return plain, plain if bits < 3 else [2, 1] + plain[2:]


def place_of(apart, owner, bits):
    even, odd = (
        sum(((apart >> b) & 1) << (bits - 2 - t) for t, b in enumerate(order)) for order in exchange_orders(bits)
    )
    return jnp.where((owner & 1) == 1, odd, even)


def packed_sums(x, alive, marks):
    segment, size = x.shape
    half = size // 2
    classes = lax.broadcasted_iota(jnp.int32, (CLASSES, segment), 0)
    hot = jnp.where((marks == classes) & alive, 1.0, 0.0)
    counts = jnp.sum(hot, axis=1, keepdims=True)
    live = jnp.where(alive, 1.0, 0.0).astype(jnp.bfloat16)
    left = jnp.concatenate([x.T * live, hot.astype(jnp.bfloat16)], axis=0)
    both = jnp.dot(left, x, preferred_element_type=jnp.float32)
    moment, sums = both[:size], both[size:]
    ci = lax.broadcasted_iota(jnp.int32, (CLASSES, half), 0)
    cj = lax.broadcasted_iota(jnp.int32, (CLASSES, half), 1)
    count_row = jnp.sum(jnp.where(ci == cj, counts, 0.0), axis=0, keepdims=True)
    i = lax.broadcasted_iota(jnp.int32, (half, half), 0)
    j = lax.broadcasted_iota(jnp.int32, (half, half), 1)
    last = moment[half:, half:]
    mixed = jnp.where(i <= j, moment[:half, :half], last)
    diagonal = jnp.sum(jnp.where(i == j, last, 0.0), axis=0, keepdims=True)
    ti = lax.broadcasted_iota(jnp.int32, (8, half), 0)
    tail = jnp.where(ti == 0, diagonal, jnp.where(ti == 1, count_row, 0.0))
    return moment[:half, half:], mixed, sums, tail


def packed_shape(size, blocks):
    return pltpu.VMEM((blocks, size + 2 * CLASSES + 8, size // 2), jnp.float32)


def fill(out, first, listed, rows, ids, marks, ready=None):
    _, segment, size = rows.shape
    half = size // 2

    def step(q, carry):
        node = listed[first + q]
        if ready is not None:
            ready(node)
        here = pl.ds(pl.multiple_of(node * segment, segment), segment)
        alive = ids[here].reshape(1, segment) == node
        cross, mixed, sums, tail = packed_sums(rows[node], alive, marks[here].reshape(1, segment))
        out[q, 0:half] = cross
        out[q, half:size] = mixed
        out[q, size : size + CLASSES] = sums[:, :half]
        out[q, size + CLASSES : size + 2 * CLASSES] = sums[:, half:]
        out[q, size + 2 * CLASSES :] = tail
        return carry

    lax.fori_loop(0, out.shape[0], step, 0)


def first_sums_kernel(
    bits, owners, features, node_ids, labels, sent, listed, rows, ids, marks, owner_list, row_sems, list_sem, id_sem, mark_sem
):
    nodes = owners.shape[0]
    blocks = sent.shape[0]
    segment = rows.shape[1]
    copies = [
        pltpu.make_async_copy(owners, owner_list, list_sem),
        pltpu.make_async_copy(node_ids, ids, id_sem),
        pltpu.make_async_copy(labels, marks, mark_sem),
    ]
    for copy in copies:
        copy.start()

    def row_copy(node):
        start = pl.multiple_of(node * segment, segment)
        return pltpu.make_async_copy(features.at[pl.ds(start, segment)], rows.at[node], row_sems.at[node])

    for node in range(nodes):
        row_copy(node).start()
    copies[0].wait()
    me = lax.axis_index("rows")
    for node in range(nodes):
        owner = owner_list[node]
        apart = owner ^ me
        place = place_of(apart, owner, bits)
        chunk = 7 - 2 * (place >> (bits - 3)) - (apart & 1)
        listed[chunk * blocks + (place & (blocks - 1))] = node
    for copy in copies[1:]:
        copy.wait()
    fill(sent, 0, listed, rows, ids, marks, lambda node: row_copy(node).wait())
    for position in range(blocks, nodes):
        row_copy(listed[position]).wait()


def hbm(x):
    return pltpu.with_memory_space_constraint(x, pltpu.HBM)


def first_sums(features, node_ids, labels, owners, bits):
    row_count, size = features.shape
    nodes = owners.shape[0]
    far = pl.BlockSpec(memory_space=pltpu.HBM)
    near = pl.BlockSpec(memory_space=pltpu.VMEM)
    words = pl.BlockSpec(memory_space=pltpu.SMEM)
    return pl.pallas_call(
        functools.partial(first_sums_kernel, bits),
        out_shape=(
            packed_shape(size, nodes // 8),
            pltpu.SMEM((nodes,), jnp.int32),
            pltpu.VMEM((nodes, row_count // nodes, size), features.dtype),
            pltpu.VMEM((row_count,), jnp.int32),
            pltpu.VMEM((row_count,), jnp.int32),
        ),
        in_specs=[far] * 4,
        out_specs=(near, words, near, near, near),
        scratch_shapes=[
            pltpu.SMEM((nodes,), jnp.int32),
            pltpu.SemaphoreType.DMA((nodes,)),
            pltpu.SemaphoreType.DMA,
            pltpu.SemaphoreType.DMA,
            pltpu.SemaphoreType.DMA,
        ],
        compiler_params=pltpu.CompilerParams(vmem_limit_bytes=32 << 20),
        name="first_sums",
    )(hbm(owners), hbm(features), hbm(node_ids), hbm(labels))


def sums_cost(shape, chunks):
    row_count, size = shape
    return pl.CostEstimate(
        flops=row_count * size * size * chunks // 4, bytes_accessed=row_count * size * chunks // 4, transcendentals=0
    )


def more_sums_kernel(chunks, listed, rows, ids, marks, *outs):
    for chunk, out in zip(chunks, outs):
        blocks = out.shape[0]
        fill(out, chunk * blocks, listed, rows, ids, marks)


def more_sums(chunks, listed, rows, ids, marks):
    size = rows.shape[2]
    nodes = listed.shape[0]
    near = pl.BlockSpec(memory_space=pltpu.VMEM)
    return pl.pallas_call(
        functools.partial(more_sums_kernel, chunks),
        out_shape=(packed_shape(size, nodes // 8),) * len(chunks),
        in_specs=[pl.BlockSpec(memory_space=pltpu.SMEM), near, near, near],
        out_specs=(near,) * len(chunks),
        compiler_params=pltpu.CompilerParams(vmem_limit_bytes=32 << 20),
        cost_estimate=sums_cost((ids.shape[0], size), len(chunks)),
        name="more_sums",
    )(listed, rows, ids, marks)


def sweep(matrix, size, columns, works):
    across = size // LANES
    lanes = lax.broadcasted_iota(jnp.int32, (1, size), 1)
    rows = lax.broadcasted_iota(jnp.int32, (PANEL, 1), 0)
    lane_id = lax.broadcasted_iota(jnp.int32, (PANEL, size), 1)
    row_id = lax.broadcasted_iota(jnp.int32, (PANEL, size), 0)
    odd = (lax.broadcasted_iota(jnp.int32, (PANEL, size), 0) & 1) == 1

    def spread(x, at):
        return jnp.broadcast_to(x[:, at : at + 1], (PANEL, LANES))

    def wide(x):
        return jnp.concatenate([x] * across, axis=1)

    panel = matrix[0:PANEL, :]
    for first in range(0, size, PANEL):
        last = first + PANEL
        inside = (lanes >= first) & (lanes < last)
        p1, p2, p3 = split(panel)
        left = jnp.concatenate([p1, p1, p2, p2, p1, p3], axis=0)
        column = [spread(panel, first + c) for c in range(PANEL)]
        if last < size:
            following = matrix[last : last + PANEL, :]
            ahead = [spread(following, first + c) for c in range(PANEL)]
        work = jnp.where(inside, jnp.where(lane_id == row_id + first, -1.0, 0.0), panel)
        own = jnp.zeros((PANEL, LANES), jnp.float32)
        cross = own
        for k in range(0, PANEL, 2):
            c0, c1 = column[k], column[k + 1]
            group, turn = k // 8 * 8, k // 2 % 2
            for c in range(k, PANEL):
                columns[turn, c, 0:8] = column[c][group : group + 8, :]
            works[turn, 0:8] = work[group : group + 8, :]

            def repeated(ref, at, group=group):
                rows8 = ref[pl.ds(at - group, 8, stride=0), :]
                return jnp.concatenate([rows8] * (PANEL // 8), axis=0)

            b00, b10 = (repeated(columns.at[turn, k], k + t) for t in range(2))
            b11 = repeated(columns.at[turn, k + 1], k + 1)
            inverse = 1.0 / (b00 * b11 - b10 * b10)
            n00, n10, n11 = b11 * inverse, -b10 * inverse, b00 * inverse
            pair = (rows == k) | (rows == k + 1)
            c0, c1 = jnp.where(pair, 0.0, c0), jnp.where(pair, 0.0, c1)
            f0, f1 = c0 * n00 + c1 * n10, c0 * n10 + c1 * n11
            own = jnp.where(rows == k, n00, jnp.where(rows == k + 1, n11, own))
            cross = jnp.where(pair, n10, cross)
            for c in range(k + 2, PANEL):
                row0, row1 = (repeated(columns.at[turn, c], k + t) for t in range(2))
                column[c] = column[c] - f0 * row0 - f1 * row1
            row0, row1 = (repeated(works.at[turn], k + t) for t in range(2))
            work = work - wide(f0) * row0 - wide(f1) * row1
        other = jnp.where(odd, pltpu.roll(work, 1, 0), pltpu.roll(work, PANEL - 1, 0))
        work = work * wide(own) + other * wide(cross)
        if last < size:
            terms = [wide(ahead[c]) * work[c : c + 1, :] for c in range(PANEL)]
            while len(terms) > 1:
                terms = [terms[t] + terms[t + 1] for t in range(0, len(terms), 2)]
            panel = jnp.where(inside, 0.0, following) - terms[0]
        w1, w2, w3 = split(work)
        right = jnp.concatenate([w1, w2, w1, w2, w3, w1], axis=0)
        starts = list(range(0, size, LANES))
        needed = last + PANEL if last + PANEL < size else 0
        for base in sorted(starts, key=lambda t: not t <= needed < t + LANES):
            part = over_rows(left[:, base : base + LANES], right)
            for lane in starts:
                block = matrix[base : base + LANES, lane : lane + LANES]
                if lane <= first < lane + LANES:
                    block = jnp.where(inside[:, lane : lane + LANES], 0.0, block)
                matrix[base : base + LANES, lane : lane + LANES] = block - part[:, lane : lane + LANES]
        matrix[first:last, :] = work


def solve_kernel(kept, came, planes, message, matrix, columns, works):
    size = matrix.shape[0]
    half = size // 2
    packed = kept[0] + came[0]
    cross, mixed = packed[:half], packed[half:size]
    sums = jnp.concatenate([packed[size : size + CLASSES], packed[size + CLASSES : size + 2 * CLASSES]], axis=1)
    at = size + 2 * CLASSES
    diagonal, count_row = packed[at : at + 1], packed[at + 1 : at + 2]
    i = lax.broadcasted_iota(jnp.int32, (half, half), 0)
    j = lax.broadcasted_iota(jnp.int32, (half, half), 1)
    ci = lax.broadcasted_iota(jnp.int32, (CLASSES, half), 0)
    cj = lax.broadcasted_iota(jnp.int32, (CLASSES, half), 1)
    counts = jnp.sum(jnp.where(ci == cj, count_row, 0.0), axis=1, keepdims=True)
    total = jnp.sum(counts, axis=0, keepdims=True)
    centers = jnp.sum(sums, axis=0, keepdims=True) / total
    scaled = sums / jnp.maximum(counts, 1.0)
    shifts = (sums - counts * centers) / total
    between = wide_over_rows(sums, scaled)
    upper = jnp.where(i < j, mixed, 0.0)
    lower = jnp.where(i > j, mixed, 0.0)
    ridge = jnp.where(i == j, RIDGE, 0.0)
    start = upper + upper.T + jnp.where(i == j, mixed, 0.0)
    end = lower + lower.T + jnp.where(i == j, diagonal, 0.0)
    matrix[:half, :half] = (start - between[:half, :half]) / total + ridge
    matrix[:half, half:] = (cross - between[:half, half:]) / total
    matrix[half:, :half] = (cross.T - between[half:, :half]) / total
    matrix[half:, half:] = (end - between[half:, half:]) / total + ridge
    sweep(matrix, size, columns, works)
    result = -jnp.dot(shifts, matrix[...], precision=HIGH, preferred_element_type=jnp.float32)
    planes[0] = result
    offsets = -jnp.sum(result * centers, axis=1, keepdims=True)
    lane = lax.broadcasted_iota(jnp.int32, (CLASSES, LANES), 1)
    parts = jnp.zeros((CLASSES, LANES), jnp.float32)
    for t, term in enumerate(split(offsets)):
        parts = jnp.where(lane == t, term.astype(jnp.float32), parts)
    message[0, :, :size] = result.astype(jnp.bfloat16)
    message[0, :, size:] = parts.astype(jnp.bfloat16)


def solve(kept, came, size):
    return pl.pallas_call(
        solve_kernel,
        out_shape=(
            jax.ShapeDtypeStruct((1, CLASSES, size), jnp.float32),
            jax.ShapeDtypeStruct((1, CLASSES, size + LANES), jnp.bfloat16),
        ),
        scratch_shapes=[
            pltpu.VMEM((size, size), jnp.float32),
            pltpu.VMEM((2, PANEL, 16, LANES), jnp.float32),
            pltpu.VMEM((2, 16, size), jnp.float32),
        ],
        compiler_params=pltpu.CompilerParams(vmem_limit_bytes=32 << 20),
        name="solve",
    )(kept, came)


def scores_kernel(parity, listed, rows, ids, messages, *refs):
    scores, scratch, sems = refs[-3:]
    nodes, segment, size = rows.shape
    blocks = nodes // 8
    copies = []
    for chunk in range(1 - parity, 8, 2):
        for q in range(blocks):
            node = listed[chunk * blocks + q]
            start = pl.multiple_of(node * segment, segment)
            alive = ids[pl.ds(start, segment)].reshape(1, segment) == node
            message = messages[(7 - chunk) // 2 * blocks + q]
            offsets = jnp.sum(message[:, size:].astype(jnp.float32), axis=1, keepdims=True)
            result = lax.dot_general(
                message[:, :size], rows[node], (((1,), (1,)), ((), ())), preferred_element_type=jnp.float32
            )
            slot = len(copies)
            scratch[slot] = jnp.where(alive, result + offsets, 0.0)
            copies.append(
                pltpu.make_async_copy(scratch.at[slot], scores.at[:, pl.ds(start, segment)], sems.at[slot])
            )
            copies[-1].start()
    for copy in copies:
        copy.wait()


def half_scores(parity, listed, rows, ids, messages, *earlier):
    nodes, segment, _ = rows.shape
    near = pl.BlockSpec(memory_space=pltpu.VMEM)
    far = pl.BlockSpec(memory_space=pltpu.HBM)
    return pl.pallas_call(
        functools.partial(scores_kernel, parity),
        out_shape=pltpu.HBM((CLASSES, nodes * segment), jnp.float32),
        in_specs=[pl.BlockSpec(memory_space=pltpu.SMEM), near, near, near] + [far] * len(earlier),
        out_specs=far,
        scratch_shapes=[
            pltpu.VMEM((nodes // 2, CLASSES, segment), jnp.float32),
            pltpu.SemaphoreType.DMA((nodes // 2,)),
        ],
        input_output_aliases={4: 0} if earlier else {},
        compiler_params=pltpu.CompilerParams(vmem_limit_bytes=32 << 20),
        name="half_scores",
    )(listed, rows, ids, messages, *(hbm(e) for e in earlier))


def on_device(ranks, features, node_ids, labels, owners):
    size = features.shape[1]
    bits = ranks.bit_length() - 1
    orders = exchange_orders(bits)

    def swap(x, distances):
        return lax.ppermute(x, "rows", [(r, r ^ distances[r & 1]) for r in range(ranks)])

    def halving(x, step):
        return swap(x, [1 << order[step] for order in orders])

    sent_a, listed, rows, ids, marks = first_sums(features, node_ids, labels, owners, bits)
    came_a = swap(sent_a, (1, 1))
    kept_a, sent_b = more_sums((1, 2), listed, rows, ids, marks)
    came_b = swap(sent_b, (1, 1))
    sent_a, listed = lax.optimization_barrier((kept_a + came_a, listed))
    came_a = halving(sent_a, 0)
    kept_b, next_a = more_sums((3, 4), listed, rows, ids, marks)
    next_a = swap(next_a, (1, 1))
    sent_b, listed = lax.optimization_barrier((kept_b + came_b, listed))
    came_b = halving(sent_b, 0)
    (kept_a,) = more_sums((5,), listed, rows, ids, marks)
    sent_a, listed = lax.optimization_barrier((kept_a + next_a + came_a, listed))
    came = halving(sent_a, 1)
    next_b, kept_b = more_sums((6, 7), listed, rows, ids, marks)
    next_b = swap(next_b, (1, 1))
    kept = (kept_b, next_b, came_b)
    for step in range(2, bits - 1):
        middle = came.shape[0] // 2
        sent = sum(k[middle:] for k in kept) + came[middle:]
        next_came = halving(sent, step)
        kept = (sum(k[:middle] for k in kept) + came[:middle],)
        came = next_came
    planes, held = solve(kept[0], came, size)
    for step in reversed(range(bits - 1)):
        held = jnp.concatenate([held, halving(held, step)], axis=0)
    others = swap(held, (1, 1))
    scores = half_scores(0, listed, rows, ids, held)
    return planes, half_scores(1, listed, rows, ids, others, scores)


def solution(mesh):
    ranks = mesh.shape["rows"]
    in_specs = (P(("leaf", "rows"), None), P(("leaf", "rows")), P(("leaf", "rows")), P("leaf"))
    out_specs = (P(("leaf", "rows"), None, None), P(None, ("leaf", "rows")))
    return jax.shard_map(
        functools.partial(on_device, ranks), mesh=mesh, in_specs=in_specs, out_specs=out_specs, check_vma=False
    )
```

```python
import functools

import jax
import jax.numpy as jnp
from jax import lax
from jax.experimental import pallas as pl
from jax.experimental.pallas import tpu as pltpu
from jax.sharding import PartitionSpec as P

CLASSES = 16
RIDGE = 0.1
PANEL = 16
LANES = 128
HIGH = lax.Precision.HIGHEST


def split(x):
    hi = x.astype(jnp.bfloat16)
    rest = x - hi.astype(jnp.float32)
    mid = rest.astype(jnp.bfloat16)
    low = (rest - mid.astype(jnp.float32)).astype(jnp.bfloat16)
    return hi, mid, low


def over_rows(a, b):
    return lax.dot_general(a, b, (((0,), (0,)), ((), ())), preferred_element_type=jnp.float32)


def wide_over_rows(a, b):
    a1, a2, a3 = split(a)
    b1, b2, b3 = split(b)
    return over_rows(
        jnp.concatenate([a1, a1, a2, a2, a1, a3], axis=0), jnp.concatenate([b1, b2, b1, b2, b3, b1], axis=0)
    )


def exchange_orders(bits):
    plain = list(range(1, bits))
    return plain, plain if bits < 3 else [2, 1] + plain[2:]


def place_of(apart, owner, bits):
    even, odd = (
        sum(((apart >> b) & 1) << (bits - 2 - t) for t, b in enumerate(order)) for order in exchange_orders(bits)
    )
    return jnp.where((owner & 1) == 1, odd, even)


def packed_sums(x, alive, marks):
    segment, size = x.shape
    half = size // 2
    classes = lax.broadcasted_iota(jnp.int32, (CLASSES, segment), 0)
    hot = jnp.where((marks == classes) & alive, 1.0, 0.0)
    counts = jnp.sum(hot, axis=1, keepdims=True)
    live = jnp.where(alive, 1.0, 0.0).astype(jnp.bfloat16)
    left = jnp.concatenate([x.T * live, hot.astype(jnp.bfloat16)], axis=0)
    both = jnp.dot(left, x, preferred_element_type=jnp.float32)
    moment, sums = both[:size], both[size:]
    ci = lax.broadcasted_iota(jnp.int32, (CLASSES, half), 0)
    cj = lax.broadcasted_iota(jnp.int32, (CLASSES, half), 1)
    count_row = jnp.sum(jnp.where(ci == cj, counts, 0.0), axis=0, keepdims=True)
    i = lax.broadcasted_iota(jnp.int32, (half, half), 0)
    j = lax.broadcasted_iota(jnp.int32, (half, half), 1)
    last = moment[half:, half:]
    mixed = jnp.where(i <= j, moment[:half, :half], last)
    diagonal = jnp.sum(jnp.where(i == j, last, 0.0), axis=0, keepdims=True)
    ti = lax.broadcasted_iota(jnp.int32, (8, half), 0)
    tail = jnp.where(ti == 0, diagonal, jnp.where(ti == 1, count_row, 0.0))
    return moment[:half, half:], mixed, sums, tail


def packed_shape(size, blocks):
    return pltpu.VMEM((blocks, size + 2 * CLASSES + 8, size // 2), jnp.float32)


def fill(out, first, listed, rows, ids, marks, ready=None):
    _, segment, size = rows.shape
    half = size // 2

    def step(q, carry):
        node = listed[first + q]
        if ready is not None:
            ready(node)
        here = pl.ds(pl.multiple_of(node * segment, segment), segment)
        alive = ids[here].reshape(1, segment) == node
        cross, mixed, sums, tail = packed_sums(rows[node], alive, marks[here].reshape(1, segment))
        out[q, 0:half] = cross
        out[q, half:size] = mixed
        out[q, size : size + CLASSES] = sums[:, :half]
        out[q, size + CLASSES : size + 2 * CLASSES] = sums[:, half:]
        out[q, size + 2 * CLASSES :] = tail
        return carry

    lax.fori_loop(0, out.shape[0], step, 0)


def first_sums_kernel(
    bits, owners, features, node_ids, labels, sent, listed, rows, ids, marks, owner_list, row_sems, list_sem, id_sem, mark_sem
):
    nodes = owners.shape[0]
    blocks = sent.shape[0]
    segment = rows.shape[1]
    copies = [
        pltpu.make_async_copy(owners, owner_list, list_sem),
        pltpu.make_async_copy(node_ids, ids, id_sem),
        pltpu.make_async_copy(labels, marks, mark_sem),
    ]
    for copy in copies:
        copy.start()

    def row_copy(node):
        start = pl.multiple_of(node * segment, segment)
        return pltpu.make_async_copy(features.at[pl.ds(start, segment)], rows.at[node], row_sems.at[node])

    for node in range(nodes):
        row_copy(node).start(priority=node % 2)
    copies[0].wait()
    me = lax.axis_index("rows")
    for node in range(nodes):
        owner = owner_list[node]
        apart = owner ^ me
        place = place_of(apart, owner, bits)
        chunk = 7 - 2 * (place >> (bits - 3)) - (apart & 1)
        listed[chunk * blocks + (place & (blocks - 1))] = node
    for copy in copies[1:]:
        copy.wait()
    fill(sent, 0, listed, rows, ids, marks, lambda node: row_copy(node).wait())
    for position in range(blocks, nodes):
        row_copy(listed[position]).wait()


def hbm(x):
    return pltpu.with_memory_space_constraint(x, pltpu.HBM)


def first_sums(features, node_ids, labels, owners, bits):
    row_count, size = features.shape
    nodes = owners.shape[0]
    far = pl.BlockSpec(memory_space=pltpu.HBM)
    near = pl.BlockSpec(memory_space=pltpu.VMEM)
    words = pl.BlockSpec(memory_space=pltpu.SMEM)
    return pl.pallas_call(
        functools.partial(first_sums_kernel, bits),
        out_shape=(
            packed_shape(size, nodes // 8),
            pltpu.SMEM((nodes,), jnp.int32),
            pltpu.VMEM((nodes, row_count // nodes, size), features.dtype),
            pltpu.VMEM((row_count,), jnp.int32),
            pltpu.VMEM((row_count,), jnp.int32),
        ),
        in_specs=[far] * 4,
        out_specs=(near, words, near, near, near),
        scratch_shapes=[
            pltpu.SMEM((nodes,), jnp.int32),
            pltpu.SemaphoreType.DMA((nodes,)),
            pltpu.SemaphoreType.DMA,
            pltpu.SemaphoreType.DMA,
            pltpu.SemaphoreType.DMA,
        ],
        compiler_params=pltpu.CompilerParams(vmem_limit_bytes=32 << 20),
        name="first_sums",
    )(hbm(owners), hbm(features), hbm(node_ids), hbm(labels))


def sums_cost(shape, chunks):
    row_count, size = shape
    return pl.CostEstimate(
        flops=row_count * size * size * chunks // 4, bytes_accessed=row_count * size * chunks // 4, transcendentals=0
    )


def more_sums_kernel(chunks, listed, rows, ids, marks, *outs):
    for chunk, out in zip(chunks, outs):
        blocks = out.shape[0]
        fill(out, chunk * blocks, listed, rows, ids, marks)


def more_sums(chunks, listed, rows, ids, marks):
    size = rows.shape[2]
    nodes = listed.shape[0]
    near = pl.BlockSpec(memory_space=pltpu.VMEM)
    return pl.pallas_call(
        functools.partial(more_sums_kernel, chunks),
        out_shape=(packed_shape(size, nodes // 8),) * len(chunks),
        in_specs=[pl.BlockSpec(memory_space=pltpu.SMEM), near, near, near],
        out_specs=(near,) * len(chunks),
        compiler_params=pltpu.CompilerParams(vmem_limit_bytes=32 << 20),
        cost_estimate=sums_cost((ids.shape[0], size), len(chunks)),
        name="more_sums",
    )(listed, rows, ids, marks)


def sweep(matrix, size, columns, works):
    across = size // LANES
    lanes = lax.broadcasted_iota(jnp.int32, (1, size), 1)
    rows = lax.broadcasted_iota(jnp.int32, (PANEL, 1), 0)
    lane_id = lax.broadcasted_iota(jnp.int32, (PANEL, size), 1)
    row_id = lax.broadcasted_iota(jnp.int32, (PANEL, size), 0)
    odd = (lax.broadcasted_iota(jnp.int32, (PANEL, size), 0) & 1) == 1

    def spread(x, at):
        return jnp.broadcast_to(x[:, at : at + 1], (PANEL, LANES))

    def wide(x):
        return jnp.concatenate([x] * across, axis=1)

    panel = matrix[0:PANEL, :]
    for first in range(0, size, PANEL):
        last = first + PANEL
        inside = (lanes >= first) & (lanes < last)
        p1, p2, p3 = split(panel)
        left = jnp.concatenate([p1, p1, p2, p2, p1, p3], axis=0)
        column = [spread(panel, first + c) for c in range(PANEL)]
        if last < size:
            following = matrix[last : last + PANEL, :]
            ahead = [spread(following, first + c) for c in range(PANEL)]
        work = jnp.where(inside, jnp.where(lane_id == row_id + first, -1.0, 0.0), panel)
        own = jnp.zeros((PANEL, LANES), jnp.float32)
        cross = own
        for k in range(0, PANEL, 2):
            c0, c1 = column[k], column[k + 1]
            group, turn = k // 8 * 8, k // 2 % 2
            for c in range(k, PANEL):
                columns[turn, c, 0:8] = column[c][group : group + 8, :]
            works[turn, 0:8] = work[group : group + 8, :]

            def repeated(ref, at, group=group):
                rows8 = ref[pl.ds(at - group, 8, stride=0), :]
                return jnp.concatenate([rows8] * (PANEL // 8), axis=0)

            b00, b10 = (repeated(columns.at[turn, k], k + t) for t in range(2))
            b11 = repeated(columns.at[turn, k + 1], k + 1)
            inverse = 1.0 / (b00 * b11 - b10 * b10)
            n00, n10, n11 = b11 * inverse, -b10 * inverse, b00 * inverse
            pair = (rows == k) | (rows == k + 1)
            c0, c1 = jnp.where(pair, 0.0, c0), jnp.where(pair, 0.0, c1)
            f0, f1 = c0 * n00 + c1 * n10, c0 * n10 + c1 * n11
            own = jnp.where(rows == k, n00, jnp.where(rows == k + 1, n11, own))
            cross = jnp.where(pair, n10, cross)
            for c in range(k + 2, PANEL):
                row0, row1 = (repeated(columns.at[turn, c], k + t) for t in range(2))
                column[c] = column[c] - f0 * row0 - f1 * row1
            row0, row1 = (repeated(works.at[turn], k + t) for t in range(2))
            work = work - wide(f0) * row0 - wide(f1) * row1
        other = jnp.where(odd, pltpu.roll(work, 1, 0), pltpu.roll(work, PANEL - 1, 0))
        work = work * wide(own) + other * wide(cross)
        if last < size:
            terms = [wide(ahead[c]) * work[c : c + 1, :] for c in range(PANEL)]
            while len(terms) > 1:
                terms = [terms[t] + terms[t + 1] for t in range(0, len(terms), 2)]
            panel = jnp.where(inside, 0.0, following) - terms[0]
        w1, w2, w3 = split(work)
        right = jnp.concatenate([w1, w2, w1, w2, w3, w1], axis=0)
        starts = list(range(0, size, LANES))
        needed = last + PANEL if last + PANEL < size else 0
        for base in sorted(starts, key=lambda t: not t <= needed < t + LANES):
            part = over_rows(left[:, base : base + LANES], right)
            for lane in starts:
                block = matrix[base : base + LANES, lane : lane + LANES]
                if lane <= first < lane + LANES:
                    block = jnp.where(inside[:, lane : lane + LANES], 0.0, block)
                matrix[base : base + LANES, lane : lane + LANES] = block - part[:, lane : lane + LANES]
        matrix[first:last, :] = work


def solve_kernel(kept, came, planes, message, matrix, columns, works):
    size = matrix.shape[0]
    half = size // 2
    packed = kept[0] + came[0]
    cross, mixed = packed[:half], packed[half:size]
    sums = jnp.concatenate([packed[size : size + CLASSES], packed[size + CLASSES : size + 2 * CLASSES]], axis=1)
    at = size + 2 * CLASSES
    diagonal, count_row = packed[at : at + 1], packed[at + 1 : at + 2]
    i = lax.broadcasted_iota(jnp.int32, (half, half), 0)
    j = lax.broadcasted_iota(jnp.int32, (half, half), 1)
    ci = lax.broadcasted_iota(jnp.int32, (CLASSES, half), 0)
    cj = lax.broadcasted_iota(jnp.int32, (CLASSES, half), 1)
    counts = jnp.sum(jnp.where(ci == cj, count_row, 0.0), axis=1, keepdims=True)
    total = jnp.sum(counts, axis=0, keepdims=True)
    centers = jnp.sum(sums, axis=0, keepdims=True) / total
    scaled = sums / jnp.maximum(counts, 1.0)
    shifts = (sums - counts * centers) / total
    between = wide_over_rows(sums, scaled)
    upper = jnp.where(i < j, mixed, 0.0)
    lower = jnp.where(i > j, mixed, 0.0)
    ridge = jnp.where(i == j, RIDGE, 0.0)
    start = upper + upper.T + jnp.where(i == j, mixed, 0.0)
    end = lower + lower.T + jnp.where(i == j, diagonal, 0.0)
    matrix[:half, :half] = (start - between[:half, :half]) / total + ridge
    matrix[:half, half:] = (cross - between[:half, half:]) / total
    matrix[half:, :half] = (cross.T - between[half:, :half]) / total
    matrix[half:, half:] = (end - between[half:, half:]) / total + ridge
    sweep(matrix, size, columns, works)
    result = -jnp.dot(shifts, matrix[...], precision=HIGH, preferred_element_type=jnp.float32)
    planes[0] = result
    offsets = -jnp.sum(result * centers, axis=1, keepdims=True)
    lane = lax.broadcasted_iota(jnp.int32, (CLASSES, LANES), 1)
    parts = jnp.zeros((CLASSES, LANES), jnp.float32)
    for t, term in enumerate(split(offsets)):
        parts = jnp.where(lane == t, term.astype(jnp.float32), parts)
    message[0, :, :size] = result.astype(jnp.bfloat16)
    message[0, :, size:] = parts.astype(jnp.bfloat16)


def solve(kept, came, size):
    return pl.pallas_call(
        solve_kernel,
        out_shape=(
            jax.ShapeDtypeStruct((1, CLASSES, size), jnp.float32),
            jax.ShapeDtypeStruct((1, CLASSES, size + LANES), jnp.bfloat16),
        ),
        scratch_shapes=[
            pltpu.VMEM((size, size), jnp.float32),
            pltpu.VMEM((2, PANEL, 16, LANES), jnp.float32),
            pltpu.VMEM((2, 16, size), jnp.float32),
        ],
        compiler_params=pltpu.CompilerParams(vmem_limit_bytes=32 << 20),
        name="solve",
    )(kept, came)


def scores_kernel(parity, listed, rows, ids, messages, *refs):
    scores, scratch, sems = refs[-3:]
    nodes, segment, size = rows.shape
    blocks = nodes // 8
    copies = []
    for chunk in range(1 - parity, 8, 2):
        for q in range(blocks):
            node = listed[chunk * blocks + q]
            start = pl.multiple_of(node * segment, segment)
            alive = ids[pl.ds(start, segment)].reshape(1, segment) == node
            message = messages[(7 - chunk) // 2 * blocks + q]
            offsets = jnp.sum(message[:, size:].astype(jnp.float32), axis=1, keepdims=True)
            result = lax.dot_general(
                message[:, :size], rows[node], (((1,), (1,)), ((), ())), preferred_element_type=jnp.float32
            )
            slot = len(copies)
            scratch[slot] = jnp.where(alive, result + offsets, 0.0)
            copies.append(
                pltpu.make_async_copy(scratch.at[slot], scores.at[:, pl.ds(start, segment)], sems.at[slot])
            )
            copies[-1].start()
    for copy in copies:
        copy.wait()


def half_scores(parity, listed, rows, ids, messages, *earlier):
    nodes, segment, _ = rows.shape
    near = pl.BlockSpec(memory_space=pltpu.VMEM)
    far = pl.BlockSpec(memory_space=pltpu.HBM)
    return pl.pallas_call(
        functools.partial(scores_kernel, parity),
        out_shape=pltpu.HBM((CLASSES, nodes * segment), jnp.float32),
        in_specs=[pl.BlockSpec(memory_space=pltpu.SMEM), near, near, near] + [far] * len(earlier),
        out_specs=far,
        scratch_shapes=[
            pltpu.VMEM((nodes // 2, CLASSES, segment), jnp.float32),
            pltpu.SemaphoreType.DMA((nodes // 2,)),
        ],
        input_output_aliases={4: 0} if earlier else {},
        compiler_params=pltpu.CompilerParams(vmem_limit_bytes=32 << 20),
        name="half_scores",
    )(listed, rows, ids, messages, *(hbm(e) for e in earlier))


def on_device(ranks, features, node_ids, labels, owners):
    size = features.shape[1]
    bits = ranks.bit_length() - 1
    orders = exchange_orders(bits)

    def swap(x, distances):
        return lax.ppermute(x, "rows", [(r, r ^ distances[r & 1]) for r in range(ranks)])

    def halving(x, step):
        return swap(x, [1 << order[step] for order in orders])

    sent_a, listed, rows, ids, marks = first_sums(features, node_ids, labels, owners, bits)
    came_a = swap(sent_a, (1, 1))
    kept_a, sent_b = more_sums((1, 2), listed, rows, ids, marks)
    came_b = swap(sent_b, (1, 1))
    sent_a, listed = lax.optimization_barrier((kept_a + came_a, listed))
    came_a = halving(sent_a, 0)
    kept_b, next_a = more_sums((3, 4), listed, rows, ids, marks)
    next_a = swap(next_a, (1, 1))
    sent_b, listed = lax.optimization_barrier((kept_b + came_b, listed))
    came_b = halving(sent_b, 0)
    (kept_a,) = more_sums((5,), listed, rows, ids, marks)
    sent_a, listed = lax.optimization_barrier((kept_a + next_a + came_a, listed))
    came = halving(sent_a, 1)
    next_b, kept_b = more_sums((6, 7), listed, rows, ids, marks)
    next_b = swap(next_b, (1, 1))
    kept = (kept_b, next_b, came_b)
    for step in range(2, bits - 1):
        middle = came.shape[0] // 2
        sent = sum(k[middle:] for k in kept) + came[middle:]
        next_came = halving(sent, step)
        kept = (sum(k[:middle] for k in kept) + came[:middle],)
        came = next_came
    planes, held = solve(kept[0], came, size)
    for step in reversed(range(bits - 1)):
        held = jnp.concatenate([held, halving(held, step)], axis=0)
    others = swap(held, (1, 1))
    scores = half_scores(0, listed, rows, ids, held)
    return planes, half_scores(1, listed, rows, ids, others, scores)


def solution(mesh):
    ranks = mesh.shape["rows"]
    in_specs = (P(("leaf", "rows"), None), P(("leaf", "rows")), P(("leaf", "rows")), P("leaf"))
    out_specs = (P(("leaf", "rows"), None, None), P(None, ("leaf", "rows")))
    return jax.shard_map(
        functools.partial(on_device, ranks), mesh=mesh, in_specs=in_specs, out_specs=out_specs, check_vma=False
    )
```
